32 devices in a mesh: wide: 16 (over z, y, x), narrow: 2 (over core).
Axes of the slice: x: 2, y: 2, z: 4, core: 2. Of those that a mesh axis runs over, the one named last changes fastest.
Arguments:
- frames: bfloat16 [4096, 1024], P('wide'), may hold values from -6 to 6
- expert_ids: int32 [4096, 2], P('wide'), may hold values from 0 to 15, all different within a row; in each aligned block of 256 rows (0 to 255, 256 to 511, ...) at most 64 rows name the same one
- gate_values: float32 [4096, 2], P('wide'), may hold values from 0.1 to 1
- w_gate: bfloat16 [16, 1024, 4096], P('wide', None, 'narrow'), may hold values from -0.1875 to 0.1875
- w_up: bfloat16 [16, 1024, 4096], P('wide', None, 'narrow'), may hold values from -0.1875 to 0.1875
- w_down: bfloat16 [16, 4096, 1024], P('wide', 'narrow'), may hold values from -0.09375 to 0.09375
- norm_gain: float32 [1024], replicated, may hold values from 0.1 to 1.9
- norm_bias: float32 [1024], replicated, may hold values from -2 to 2
- point_in: bfloat16 [1024, 2, 1024], P(None, None, 'narrow'), may hold values from -0.1875 to 0.1875
- depth_kernel: bfloat16 [31, 1024], P(None, 'narrow'), may hold values from -1 to 1
- point_out: bfloat16 [1024, 1024], P('narrow'), may hold values from -0.1875 to 0.1875
Outputs:
- block_out: bfloat16 [4096, 1024], P(('wide', 'narrow'))
The draws below stay inside these ranges and needn't reach their ends.
Inputs may be any that keep to these rules, and one draw needn't show every extreme that they name: `expert_ids`: each frame names 2 different experts; in each aligned block of 256 frames no expert is named by more than 64 frames, and every expert is named somewhere.
All inputs are finite; a program needn't handle non-finite values.
Results may differ from the reference program's by a relative error of at most 0.015.
Values may be sent and summed in bfloat16 or wider, within the bound.
A program may use at most 64 MiB of HBM per device.

```python
import math
import jax
import jax.numpy as jnp
import numpy as np
from jax import lax

D = 1024
FF = 4096
TOP = 2
KERNEL = 31
TOK_GRP = 256
EXPERTS = 16
TOKENS = 4096
CAP = 64
N_WIDE = 16
N_NARROW = 2


def block_scale(key, dims, cuts, low, high):
    loudness = 1.0
    for dim, shards_of in cuts:
        draws = jax.random.uniform(jax.random.fold_in(jax.random.fold_in(key, 6), dim), (shards_of,), jnp.float32, low / len(cuts), high / len(cuts))
        loudness = loudness * jnp.repeat(jnp.exp(draws), dims[dim] // shards_of).reshape((-1,) + (1,) * (len(dims) - 1 - dim))
    return loudness


def routed_block(key, own, number, rows, count, top, reach, skew):
    sequence = jax.random.permutation(key, count)
    heavy_load, usual = portions_of(count, rows * top, reach, skew, True), portions_of(count, rows * top, reach, skew, False)
    places = jnp.arange(count)

    def named(tallies, turn):
        used = int((tallies > 0).sum())
        fixed = max(1, used // 4)
        moved = fixed + (places - fixed + turn * (used - fixed)) % max(1, count - fixed)
        return jnp.zeros((count,), jnp.int32).at[sequence[jnp.where(places < fixed, places, moved)]].set(jnp.asarray(tallies, jnp.int32))

    tallies = jnp.where(number % 4 == 0, named(heavy_load, number // 4), named(usual, number - number // 4 - 1))
    mixed = jax.random.permutation(jax.random.fold_in(own, 3), count)
    source_of, sink = mixed[0:count // 2 * 2:2], mixed[1:count // 2 * 2:2]
    slack = jnp.minimum(tallies[source_of] - 1, reach - tallies[sink]) // 2
    slack = jnp.where((source_of == sequence[0]) | (sink == sequence[0]) | (tallies[sink] == 0), 0, jnp.maximum(slack, 0))
    moved = jax.random.randint(jax.random.fold_in(own, 4), (count // 2,), 0, 1 << 20) % (slack + 1)
    tallies = tallies.at[source_of].add(-moved).at[sink].add(moved)
    items = jnp.searchsorted(jnp.cumsum(tallies), jnp.arange(rows * top), side="right").astype(jnp.int32)
    grid = items.reshape(top, rows).T
    grid = grid[jax.random.permutation(jax.random.fold_in(own, 1), rows)]
    turn = jax.random.randint(jax.random.fold_in(own, 2), (rows, 1), 0, top)
    return jnp.take_along_axis(grid, (jnp.arange(top)[None, :] + turn) % top, axis=1)


def portions_of(amount, total, bound, slope, full):
    weights = [(1 << 20) // math.isqrt(standing ** slope) + 1 for standing in range(1, amount + 1)]
    largest = bound if full else min(bound, max(-(-total // amount), total * weights[0] // sum(weights)))
    least = 1 if total - largest >= amount - 1 else 0
    holding, rest = [largest] + [least] * (amount - 1), total - largest - least * (amount - 1)
    while rest > 0:
        movable = [i for i in range(1, amount) if holding[i] < largest] or [i for i in range(1, amount) if holding[i] < bound]
        mass, left = sum([weights[i] for i in movable]), rest
        for i in movable:
            extra = min(bound - holding[i], max(1, left * weights[i] // mass), rest)
            holding[i] = holding[i] + extra
            rest = rest - extra
    return np.array(holding)


def centred(stream_key, dims, deviation, bound, shards=(), kind=jnp.bfloat16):
    result = deviation * jax.random.normal(stream_key, dims, jnp.float32)
    if shards:
        result = result * block_scale(stream_key, dims, shards, -0.22, 0.18)
    return jnp.clip(result, -bound, bound).astype(kind)


def setup_inputs(seed: int = 0) -> dict:
    key_of = jax.random.split(jax.random.key(seed), 12)
    frames = centred(key_of[0], (TOKENS, D), 1.0, 6.0, ((0, 16),))
    expert_ids_keys = jax.random.split(jax.random.fold_in(key_of[1], 1), TOKENS // TOK_GRP)
    expert_ids_turns = jax.random.permutation(jax.random.fold_in(key_of[1], 3), TOKENS // TOK_GRP)
    expert_ids = jax.vmap(lambda own, number: routed_block(jax.random.fold_in(key_of[1], 2), own, number, TOK_GRP, EXPERTS, TOP, CAP, 2))(expert_ids_keys, expert_ids_turns).reshape((TOKENS, TOP))
    gate_values = jnp.clip(0.1 + 0.9 * jax.random.uniform(key_of[2], (TOKENS, TOP), jnp.float32) ** block_scale(key_of[2], (TOKENS, TOP), ((0, 16),), -0.2, 0.2), 0.1, 1.0)
    w_gate = centred(key_of[3], (EXPERTS, D, FF), D ** -0.5, 0.1875, ((0, 16), (2, 2)))
    w_up = centred(key_of[4], (EXPERTS, D, FF), D ** -0.5, 0.1875, ((0, 16), (2, 2)))
    w_down = centred(key_of[5], (EXPERTS, FF, D), FF ** -0.5, 0.09375, ((0, 16), (1, 2)))
    norm_gain = jnp.clip(1.0 + 0.18 * jax.random.normal(key_of[6], (D,), jnp.float32), 0.1, 1.9)
    norm_bias = centred(key_of[7], (D,), 0.3, 2.0, (), jnp.float32)
    point_in = centred(key_of[8], (D, 2, D), D ** -0.5, 0.1875, ((2, 2),))
    depth_kernel = centred(key_of[9], (KERNEL, D), KERNEL ** -0.5, 1.0, ((1, 2),))
    point_out = centred(key_of[10], (D, D), D ** -0.5, 0.1875, ((0, 2),))
    return {"frames": frames, "expert_ids": expert_ids, "gate_values": gate_values, "w_gate": w_gate, "w_up": w_up, "w_down": w_down, "norm_gain": norm_gain, "norm_bias": norm_bias, "point_in": point_in, "depth_kernel": depth_kernel, "point_out": point_out}


def reference(frames, expert_ids, gate_values, w_gate, w_up, w_down, norm_gain, norm_bias, point_in, depth_kernel, point_out):
    total_rows = frames.shape[0]
    model_width = frames.shape[1]
    top_count = expert_ids.shape[1]
    grouped = expert_ids.reshape(N_WIDE, TOK_GRP * top_count)
    one_hot = (grouped[:, :, None] == jnp.arange(EXPERTS, dtype=jnp.int32)[None, None, :]).astype(jnp.int32)
    running = jnp.cumsum(one_hot, axis=1)
    slot_index = lax.optimization_barrier(jnp.sum((running - 1) * one_hot, axis=2))
    column = (jnp.arange(N_WIDE, dtype=jnp.int32)[:, None] * CAP + slot_index).reshape(-1).astype(jnp.int32)
    flat_ids = expert_ids.reshape(-1)
    token_index = (jnp.arange(total_rows * top_count, dtype=jnp.int32) // top_count).astype(jnp.int32)
    index_table = jnp.full((EXPERTS, N_WIDE * CAP), total_rows, jnp.int32).at[flat_ids, column].set(token_index)
    gate_table = jnp.zeros((EXPERTS, N_WIDE * CAP), jnp.float32).at[flat_ids, column].set(gate_values.reshape(-1).astype(jnp.float32))
    padded_frames = jnp.concatenate([frames, jnp.zeros((1, model_width), frames.dtype)], 0)
    block_size = FF // N_NARROW

    def one_expert(moe_sum, expert_index):
        picked = jnp.take(padded_frames, index_table[expert_index], axis=0)
        gate_all = w_gate[expert_index]
        up_all = w_up[expert_index]
        down_all = w_down[expert_index]
        output = jnp.zeros((N_WIDE * CAP, model_width), jnp.float32)
        for block_index in range(N_NARROW):
            low = block_index * block_size
            high = low + block_size
            gate_part = jnp.dot(picked, gate_all[:, low:high], preferred_element_type=jnp.float32)
            up_part = jnp.dot(picked, up_all[:, low:high], preferred_element_type=jnp.float32)
            hidden = (jax.nn.silu(gate_part) * up_part).astype(jnp.bfloat16)
            partial_value = jnp.dot(hidden, down_all[low:high, :], preferred_element_type=jnp.float32).astype(jnp.bfloat16)
            partial_value = lax.optimization_barrier(partial_value)
            output = output + partial_value.astype(jnp.float32)
        moe_sum = moe_sum.at[index_table[expert_index]].add(gate_table[expert_index][:, None] * output)
        return (moe_sum, None)
    moe_sum, _ = lax.scan(one_expert, jnp.zeros((total_rows + 1, model_width), jnp.float32), jnp.arange(EXPERTS, dtype=jnp.int32))
    residual = frames.astype(jnp.float32) + moe_sum[:total_rows]
    row_mean = lax.optimization_barrier(jnp.mean(residual, axis=1, keepdims=True))
    centered = residual - row_mean
    row_var = lax.optimization_barrier(jnp.mean(centered * centered, axis=1, keepdims=True))
    normed = (centered / jnp.sqrt(row_var + 1e-05) * norm_gain[None, :] + norm_bias[None, :]).astype(jnp.bfloat16)
    value_half = jnp.dot(normed, point_in[:, 0, :], preferred_element_type=jnp.float32)
    gate_half = jnp.dot(normed, point_in[:, 1, :], preferred_element_type=jnp.float32)
    glu_out = (value_half * jax.nn.sigmoid(gate_half)).astype(jnp.bfloat16)
    half_width = (KERNEL - 1) // 2
    padded = jnp.pad(glu_out, ((half_width, half_width), (0, 0)))
    depthwise = jnp.zeros((total_rows, model_width), jnp.float32)
    for tap_index in range(KERNEL):
        depthwise = depthwise + padded[tap_index:tap_index + total_rows].astype(jnp.float32) * depth_kernel[tap_index].astype(jnp.float32)[None, :]
    activated = (depthwise * jax.nn.sigmoid(depthwise)).astype(jnp.bfloat16)
    return (residual + jnp.dot(activated, point_out, preferred_element_type=jnp.float32)).astype(jnp.bfloat16)
```

```python
import functools

import jax
import jax.numpy as jnp
from jax import lax
from jax.experimental import pallas as pl
from jax.experimental.pallas import tpu as pltpu
from jax.sharding import PartitionSpec as P

F32 = jnp.float32
BF16 = jnp.bfloat16
HALO = 16


def block_kernel(
    wide,
    narrow,
    groups,
    cap,
    frames_ref,
    ids_ref,
    gates_ref,
    gain_ref,
    bias_ref,
    depth_ref,
    w_gate_hbm,
    w_up_hbm,
    w_down_hbm,
    pin_hbm,
    pout_hbm,
    out_ref,
    w_gate,
    w_up,
    w_down,
    pin,
    pout,
    outgoing,
    arrived,
    hidden,
    partial,
    partial_in,
    sums,
    returned,
    mix0,
    mix1,
    mixed,
    residual,
    padded,
    padded32,
    activated,
    shares,
    shares_in,
    w_sem,
    fs,
    fr,
    xs,
    xr,
    ps,
    pr,
    rs,
    rr,
    ms,
    mr,
    hs,
    hr,
    os_,
    or_,
):
    me_w = lax.axis_index("wide")
    me_n = lax.axis_index("narrow")
    frame_count, width = frames_ref.shape
    dc = width // narrow
    size = wide // groups
    rows = size * cap
    plane = me_w // size
    inner = me_w % size
    units = w_gate.shape[1]
    channels = pout.shape[0]
    share = frame_count // narrow
    taps = depth_ref.shape[0]

    def cols(index):
        return pl.ds(pl.multiple_of(index * dc, 128), dc)

    def slots(index):
        return pl.ds(pl.multiple_of(index * cap, 16), cap)

    def group_rows(index):
        return pl.ds(pl.multiple_of(index * rows, 16), rows)

    def share_rows(index):
        return pl.ds(pl.multiple_of(index * share, 16), share)

    my_cols = cols(me_n)

    barrier = pltpu.get_barrier_semaphore()

    def greet(i, carry):
        pl.semaphore_signal(
            barrier,
            inc=1,
            device_id=((me_w + i) % wide, me_n),
            device_id_type=pl.DeviceIdType.MESH,
        )
        return carry

    lax.fori_loop(1, wide, greet, 0)
    for i in range(1, narrow):
        pl.semaphore_signal(
            barrier,
            inc=1,
            device_id=(me_w, (me_n + i) % narrow),
            device_id_type=pl.DeviceIdType.MESH,
        )

    loads = [
        pltpu.make_async_copy(w_gate_hbm.at[0], w_gate, w_sem.at[0]),
        pltpu.make_async_copy(w_up_hbm.at[0], w_up, w_sem.at[1]),
        pltpu.make_async_copy(w_down_hbm.at[0], w_down, w_sem.at[2]),
        pltpu.make_async_copy(pin_hbm, pin, w_sem.at[3]),
        pltpu.make_async_copy(pout_hbm, pout, w_sem.at[4]),
    ]
    for load in loads:
        load.start()

    def remote(src, dst, send, recv, device):
        return pltpu.make_async_remote_copy(
            src_ref=src,
            dst_ref=dst,
            send_sem=send,
            recv_sem=recv,
            device_id=device,
            device_id_type=pl.DeviceIdType.MESH,
        )

    id0 = ids_ref[:, 0:1]
    id1 = ids_ref[:, 1:2]
    lane = lax.broadcasted_iota(jnp.int32, (frame_count, 128), 1)
    named0 = lane == id0
    named1 = lane == id1
    named = jnp.where(named0 | named1, 1.0, 0.0).astype(BF16)
    earlier = jnp.where(
        lax.broadcasted_iota(jnp.int32, (frame_count, frame_count), 0)
        > lax.broadcasted_iota(jnp.int32, (frame_count, frame_count), 1),
        1.0,
        0.0,
    ).astype(BF16)
    position = jnp.dot(earlier, named, preferred_element_type=F32)
    slot0 = id0.astype(F32) * cap + jnp.sum(
        jnp.where(named0, position, 0.0), axis=1, keepdims=True
    )
    slot1 = id1.astype(F32) * cap + jnp.sum(
        jnp.where(named1, position, 0.0), axis=1, keepdims=True
    )
    both = jnp.where(lane == 0, slot0, jnp.where(lane == 1, slot1, 0.0))
    turned = jnp.transpose(both).astype(jnp.int32)
    row0 = turned[0:1, :]
    row1 = turned[1:2, :]
    slot0 = slot0.astype(jnp.int32)
    slot1 = slot1.astype(jnp.int32)

    def send_copy(p):
        return remote(
            outgoing.at[slots(p), :],
            arrived.at[slots(me_w), my_cols],
            fs.at[p],
            fr.at[me_w],
            (p, me_n),
        )

    def recv_copy(s):
        return remote(
            outgoing.at[slots(s), :],
            arrived.at[slots(s), my_cols],
            fs.at[s],
            fr.at[s],
            (s, me_n),
        )

    mine = frames_ref[:, my_cols]
    for g in range(groups):
        q = (plane + g) % groups
        place = lax.broadcasted_iota(jnp.int32, (rows, frame_count), 0) + q * rows
        choose = jnp.where((place == row0) | (place == row1), 1.0, 0.0).astype(BF16)
        outgoing[group_rows(q), :] = jnp.dot(
            choose, mine, preferred_element_type=F32
        ).astype(BF16)
        if g == 0:
            arrived[slots(me_w), my_cols] = outgoing[slots(me_w), :]
            pl.semaphore_wait(barrier, wide - 1 + narrow - 1)

        def send(i, carry, q=q):
            send_copy(q * size + (inner + i) % size).start()
            return carry

        lax.fori_loop(1 if g == 0 else 0, size, send, 0)

    def forward_copy(g, q, m):
        part = arrived.at[group_rows(q), my_cols]
        return remote(part, part, xs.at[g, m], xr.at[g, me_n], (me_w, m))

    def forward_in(g, q, m):
        part = arrived.at[group_rows(q), cols(m)]
        return remote(part, part, xs.at[g, m], xr.at[g, m], (me_w, m))

    def partial_copy(g, q, m):
        return remote(
            partial.at[group_rows(q), cols(m)],
            partial_in.at[me_n, group_rows(q), :],
            ps.at[g, m],
            pr.at[g, me_n],
            (me_w, m),
        )

    def partial_wait(g, q, m):
        return remote(
            partial.at[group_rows(q), cols(m)],
            partial_in.at[m, group_rows(q), :],
            ps.at[g, m],
            pr.at[g, m],
            (me_w, m),
        )

    def return_copy(s):
        return remote(
            sums.at[slots(s), :],
            returned.at[slots(me_w), :],
            rs.at[s],
            rr.at[me_w],
            (s, me_n),
        )

    def return_wait(p):
        return remote(
            sums.at[slots(p), :],
            returned.at[slots(p), :],
            rs.at[p],
            rr.at[p],
            (p, me_n),
        )

    siblings = [(me_n + i) % narrow for i in range(1, narrow)]
    tile = min(512, units)

    def step(g, carry):
        q = (plane + groups - g) % groups

        def take(i, c):
            s = q * size + (inner + size - i) % size

            @pl.when(s != me_w)
            def _():
                recv_copy(s).wait_recv()

            return c

        lax.fori_loop(0, size, take, 0)
        for m in siblings:
            forward_copy(g, q, m).start()

        @pl.when(g == 0)
        def _():
            for load in loads[:3]:
                load.wait()

        for m in siblings:
            forward_in(g, q, m).wait_recv()

        x = arrived[group_rows(q), :]
        for f in range(0, units, tile):
            gate = jnp.dot(x, w_gate[:, f : f + tile], preferred_element_type=F32)
            up = jnp.dot(x, w_up[:, f : f + tile], preferred_element_type=F32)
            hidden[:, f : f + tile] = (gate * jax.nn.sigmoid(gate) * up).astype(BF16)
        for m in siblings:
            partial[group_rows(q), cols(m)] = jnp.dot(
                hidden[...], w_down[:, cols(m)], preferred_element_type=F32
            ).astype(BF16)
            partial_copy(g, q, m).start()
        total = jnp.dot(hidden[...], w_down[:, my_cols], preferred_element_type=F32)
        for m in siblings:
            partial_wait(g, q, m).wait_recv()
            total = total + partial_in[m, group_rows(q), :].astype(F32)
        sums[group_rows(q), :] = total.astype(BF16)

        def give(i, c):
            s = q * size + (inner + size - i) % size

            @pl.when(s != me_w)
            def _():
                return_copy(s).start()

            return c

        lax.fori_loop(0, size, give, 0)
        return carry

    lax.fori_loop(0, groups, step, 0)
    returned[slots(me_w), :] = sums[slots(me_w), :]

    mix0[...] = jnp.zeros_like(mix0)
    mix1[...] = jnp.zeros_like(mix1)

    def combine(g, carry):
        q = (plane + g) % groups

        def take(i, c):
            p = q * size + (inner + i) % size

            @pl.when(p != me_w)
            def _():
                return_wait(p).wait_recv()

            return c

        lax.fori_loop(0, size, take, 0)
        place = lax.broadcasted_iota(jnp.int32, (frame_count, rows), 1) + q * rows
        block = returned[group_rows(q), :]
        mix0[...] += jnp.dot(
            jnp.where(place == slot0, 1.0, 0.0).astype(BF16), block, preferred_element_type=F32
        )
        mix1[...] += jnp.dot(
            jnp.where(place == slot1, 1.0, 0.0).astype(BF16), block, preferred_element_type=F32
        )
        return carry

    lax.fori_loop(0, groups, combine, 0)
    mixed[:, my_cols] = (
        gates_ref[:, 0:1] * mix0[...] + gates_ref[:, 1:2] * mix1[...]
    ).astype(BF16)

    def mix_copy(m):
        part = mixed.at[:, my_cols]
        return remote(part, part, ms.at[m], mr.at[me_n], (me_w, m))

    def mix_wait(m):
        part = mixed.at[:, cols(m)]
        return remote(part, part, ms.at[m], mr.at[m], (me_w, m))

    for m in siblings:
        mix_copy(m).start()
    for load in loads[3:]:
        load.wait()
    for m in siblings:
        mix_wait(m).wait_recv()

    res = frames_ref[...].astype(F32) + mixed[...].astype(F32)
    residual[...] = res
    centered = res - jnp.mean(res, axis=1, keepdims=True)
    variance = jnp.mean(centered * centered, axis=1, keepdims=True)
    normed = (centered * lax.rsqrt(variance + 1e-05) * gain_ref[...] + bias_ref[...]).astype(BF16)
    value_half = jnp.dot(normed, pin[:, :channels], preferred_element_type=F32)
    gate_half = jnp.dot(normed, pin[:, channels:], preferred_element_type=F32)
    glu = (value_half * jax.nn.sigmoid(gate_half)).astype(BF16)
    padded[HALO : HALO + frame_count, :] = glu
    padded32[HALO : HALO + frame_count, :] = glu.astype(F32)

    end = HALO + frame_count
    to_left = remote(
        padded.at[HALO : 2 * HALO, :],
        padded.at[end : end + HALO, :],
        hs.at[0],
        hr.at[0],
        ((me_w + wide - 1) % wide, me_n),
    )
    to_right = remote(
        padded.at[frame_count:end, :],
        padded.at[0:HALO, :],
        hs.at[1],
        hr.at[1],
        ((me_w + 1) % wide, me_n),
    )
    has_left = me_w > 0
    has_right = me_w < wide - 1

    @pl.when(has_left)
    def _():
        to_left.start()

    @pl.when(has_right)
    def _():
        to_right.start()

    half = (taps - 1) // 2
    step_rows = 64

    def depthwise(starts):
        def strip(c, carry):
            lanes = pl.ds(pl.multiple_of(c * 128, 128), 128)
            kernel_taps = depth_ref[:, lanes].astype(F32)
            for start in starts:
                total = jnp.zeros((step_rows, 128), F32)
                for j in range(taps):
                    low = start + HALO - half + j
                    total = total + padded32[low : low + step_rows, lanes] * kernel_taps[j : j + 1, :]
                activated[start : start + step_rows, lanes] = (
                    total * jax.nn.sigmoid(total)
                ).astype(BF16)
            return carry

        lax.fori_loop(0, channels // 128, strip, 0)

    depthwise(range(step_rows, frame_count - step_rows, step_rows))

    @pl.when(has_right)
    def _():
        to_left.wait_recv()
        padded32[end : end + HALO, :] = padded[end : end + HALO, :].astype(F32)

    @pl.when(jnp.logical_not(has_right))
    def _():
        padded32[end : end + HALO, :] = jnp.zeros((HALO, channels), F32)

    @pl.when(has_left)
    def _():
        to_right.wait_recv()
        padded32[0:HALO, :] = padded[0:HALO, :].astype(F32)

    @pl.when(jnp.logical_not(has_left))
    def _():
        padded32[0:HALO, :] = jnp.zeros((HALO, channels), F32)

    depthwise((0, frame_count - step_rows))

    def share_copy(m):
        return remote(
            shares.at[share_rows(m), :], shares_in.at[me_n], os_.at[m], or_.at[me_n], (me_w, m)
        )

    def share_wait(m):
        return remote(
            shares.at[share_rows(m), :], shares_in.at[m], os_.at[m], or_.at[m], (me_w, m)
        )

    for m in siblings:
        shares[share_rows(m), :] = jnp.dot(
            activated[share_rows(m), :], pout[...], preferred_element_type=F32
        ).astype(BF16)
        share_copy(m).start()
    total = residual[share_rows(me_n), :] + jnp.dot(
        activated[share_rows(me_n), :], pout[...], preferred_element_type=F32
    )
    for m in siblings:
        share_wait(m).wait_recv()
        total = total + shares_in[m].astype(F32)
    out_ref[...] = total.astype(BF16)

    def finish(i, carry):
        p = (me_w + i) % wide
        send_copy(p).wait_send()
        return_copy(p).wait_send()
        return carry

    lax.fori_loop(1, wide, finish, 0)
    for m in siblings:
        mix_copy(m).wait_send()
        share_copy(m).wait_send()

    def finish_group(g, carry):
        q = (plane + groups - g) % groups
        for m in siblings:
            forward_copy(g, q, m).wait_send()
            partial_copy(g, q, m).wait_send()
        return carry

    lax.fori_loop(0, groups, finish_group, 0)

    @pl.when(has_left)
    def _():
        to_left.wait_send()

    @pl.when(has_right)
    def _():
        to_right.wait_send()


def shards(
    frames,
    expert_ids,
    gate_values,
    w_gate,
    w_up,
    w_down,
    norm_gain,
    norm_bias,
    point_in,
    depth_kernel,
    point_out,
):
    frame_count, width = frames.shape
    top_count = expert_ids.shape[1]
    wide = lax.axis_size("wide")
    narrow = lax.axis_size("narrow")
    expert_count = w_gate.shape[0] * wide
    cap = 2 * top_count * frame_count // expert_count
    units = w_gate.shape[2]
    channels = point_in.shape[2]
    groups = 4
    slot_count = wide * cap
    rows = slot_count // groups
    dc = width // narrow
    share = frame_count // narrow
    vmem = pl.BlockSpec(memory_space=pltpu.VMEM)
    hbm = pl.BlockSpec(memory_space=pl.ANY)
    dma = pltpu.SemaphoreType.DMA
    flops = 2 * width * (3 * slot_count * units + 3 * frame_count * channels)
    return pl.pallas_call(
        functools.partial(block_kernel, wide, narrow, groups, cap),
        out_shape=jax.ShapeDtypeStruct((share, width), BF16),
        in_specs=[vmem] * 6 + [hbm] * 5,
        out_specs=vmem,
        scratch_shapes=[
            pltpu.VMEM((width, units), BF16),
            pltpu.VMEM((width, units), BF16),
            pltpu.VMEM((units, width), BF16),
            pltpu.VMEM((width, 2 * channels), BF16),
            pltpu.VMEM((channels, width), BF16),
            pltpu.VMEM((slot_count, dc), BF16),
            pltpu.VMEM((slot_count, width), BF16),
            pltpu.VMEM((rows, units), BF16),
            pltpu.VMEM((slot_count, width), BF16),
            pltpu.VMEM((narrow, slot_count, dc), BF16),
            pltpu.VMEM((slot_count, dc), BF16),
            pltpu.VMEM((slot_count, dc), BF16),
            pltpu.VMEM((frame_count, dc), F32),
            pltpu.VMEM((frame_count, dc), F32),
            pltpu.VMEM((frame_count, width), BF16),
            pltpu.VMEM((frame_count, width), F32),
            pltpu.VMEM((frame_count + 2 * HALO, channels), BF16),
            pltpu.VMEM((frame_count + 2 * HALO, channels), F32),
            pltpu.VMEM((frame_count, channels), BF16),
            pltpu.VMEM((frame_count, width), BF16),
            pltpu.VMEM((narrow, share, width), BF16),
            dma((5,)),
            dma((wide,)),
            dma((wide,)),
            dma((groups, narrow)),
            dma((groups, narrow)),
            dma((groups, narrow)),
            dma((groups, narrow)),
            dma((wide,)),
            dma((wide,)),
            dma((narrow,)),
            dma((narrow,)),
            dma((2,)),
            dma((2,)),
            dma((narrow,)),
            dma((narrow,)),
        ],
        compiler_params=pltpu.CompilerParams(
            collective_id=0, has_side_effects=True, vmem_limit_bytes=56 * 1024 * 1024
        ),
        cost_estimate=pl.CostEstimate(
            flops=flops, bytes_accessed=2 * 3 * width * units, transcendentals=0
        ),
        name="conformer_block",
    )(
        frames,
        expert_ids,
        gate_values,
        norm_gain.reshape(1, width),
        norm_bias.reshape(1, width),
        depth_kernel,
        w_gate,
        w_up,
        w_down,
        point_in.reshape(width, 2 * channels),
        point_out,
    )


def solution(mesh):
    return jax.shard_map(
        shards,
        mesh=mesh,
        in_specs=(
            P("wide", None),
            P("wide", None),
            P("wide", None),
            P("wide", None, "narrow"),
            P("wide", None, "narrow"),
            P("wide", "narrow", None),
            P(),
            P(),
            P(None, None, "narrow"),
            P(None, "narrow"),
            P("narrow", None),
        ),
        out_specs=P(("wide", "narrow"), None),
        check_vma=False,
    )
```

```python
import functools

import jax
import jax.numpy as jnp
from jax import lax
from jax.experimental import pallas as pl
from jax.experimental.pallas import tpu as pltpu
from jax.sharding import PartitionSpec as P

F32 = jnp.float32
BF16 = jnp.bfloat16
HALO = 16


def block_kernel(
    wide,
    narrow,
    groups,
    cap,
    frames_ref,
    ids_ref,
    gates_ref,
    gain_ref,
    bias_ref,
    depth_ref,
    w_gate_hbm,
    w_up_hbm,
    w_down_hbm,
    pin_hbm,
    pout_hbm,
    out_ref,
    w_gate,
    w_up,
    w_down,
    pin_raw,
    pin,
    pout,
    turned,
    outgoing,
    arrived,
    hidden,
    partial,
    partial_in,
    sums,
    returned,
    mix0,
    mix1,
    mixed,
    residual,
    padded,
    padded32,
    activated,
    shares,
    shares_in,
    w_sem,
    fs,
    fr,
    xs,
    xr,
    ps,
    pr,
    rs,
    rr,
    ms,
    mr,
    hs,
    hr,
    os_,
    or_,
):
    me_w = lax.axis_index("wide")
    me_n = lax.axis_index("narrow")
    frame_count, width = frames_ref.shape
    dc = width // narrow
    size = wide // groups
    rows = size * cap
    plane = me_w // size
    inner = me_w % size
    units = w_gate.shape[1]
    channels = pout.shape[0]
    share = frame_count // narrow
    taps = depth_ref.shape[0]

    def cols(index):
        return pl.ds(pl.multiple_of(index * dc, 128), dc)

    def slots(index):
        return pl.ds(pl.multiple_of(index * cap, 16), cap)

    def group_rows(index):
        return pl.ds(pl.multiple_of(index * rows, 16), rows)

    def share_rows(index):
        return pl.ds(pl.multiple_of(index * share, 16), share)

    my_cols = cols(me_n)

    barrier = pltpu.get_barrier_semaphore()

    def greet(i, carry):
        pl.semaphore_signal(
            barrier,
            inc=1,
            device_id=((me_w + i) % wide, me_n),
            device_id_type=pl.DeviceIdType.MESH,
        )
        return carry

    lax.fori_loop(1, wide, greet, 0)
    for i in range(1, narrow):
        pl.semaphore_signal(
            barrier,
            inc=1,
            device_id=(me_w, (me_n + i) % narrow),
            device_id_type=pl.DeviceIdType.MESH,
        )

    loads = [
        pltpu.make_async_copy(w_gate_hbm.at[0], w_gate, w_sem.at[0]),
        pltpu.make_async_copy(w_up_hbm.at[0], w_up, w_sem.at[1]),
        pltpu.make_async_copy(w_down_hbm.at[0], w_down, w_sem.at[2]),
        pltpu.make_async_copy(pin_hbm, pin_raw, w_sem.at[3]),
        pltpu.make_async_copy(pout_hbm, pout, w_sem.at[4]),
    ]
    for load in loads:
        load.start()

    def remote(src, dst, send, recv, device):
        return pltpu.make_async_remote_copy(
            src_ref=src,
            dst_ref=dst,
            send_sem=send,
            recv_sem=recv,
            device_id=device,
            device_id_type=pl.DeviceIdType.MESH,
        )

    id0 = ids_ref[0:1, :]
    id1 = ids_ref[1:2, :]
    lane = lax.broadcasted_iota(jnp.int32, (128, frame_count), 0)
    named0 = lane == id0
    named1 = lane == id1
    named = jnp.where(named0 | named1, 1.0, 0.0).astype(BF16)
    earlier = jnp.where(
        lax.broadcasted_iota(jnp.int32, (frame_count, frame_count), 0)
        < lax.broadcasted_iota(jnp.int32, (frame_count, frame_count), 1),
        1.0,
        0.0,
    ).astype(BF16)
    position = jnp.dot(named, earlier, preferred_element_type=F32)
    row0 = id0.astype(F32) * cap + jnp.sum(
        jnp.where(named0, position, 0.0), axis=0, keepdims=True
    )
    row1 = id1.astype(F32) * cap + jnp.sum(
        jnp.where(named1, position, 0.0), axis=0, keepdims=True
    )
    stacked = jnp.where(
        lane == 0,
        row0,
        jnp.where(
            lane == 1, row1, jnp.where(lane == 2, gates_ref[0:1, :], gates_ref[1:2, :])
        ),
    )
    turned[...] = jnp.transpose(stacked)
    row0 = row0.astype(jnp.int32)
    row1 = row1.astype(jnp.int32)

    def plane_of(g):
        return ((plane // 2 + g % 2) % 2) * 2 + (plane % 2 + g // 2) % 2

    def send_copy(p):
        return remote(
            outgoing.at[slots(p), :],
            arrived.at[slots(me_w), my_cols],
            fs.at[p],
            fr.at[me_w],
            (p, me_n),
        )

    def recv_copy(s):
        return remote(
            outgoing.at[slots(s), :],
            arrived.at[slots(s), my_cols],
            fs.at[s],
            fr.at[s],
            (s, me_n),
        )

    mine = frames_ref[:, my_cols]
    for turn, g in enumerate((1, 0, 3, 2)):
        q = plane_of(g)
        place = lax.broadcasted_iota(jnp.int32, (rows, frame_count), 0) + q * rows
        choose = jnp.where((place == row0) | (place == row1), 1.0, 0.0).astype(BF16)
        outgoing[group_rows(q), :] = jnp.dot(
            choose, mine, preferred_element_type=F32
        ).astype(BF16)
        if turn == 0:
            pl.semaphore_wait(barrier, wide - 1 + narrow - 1)
        if g == 0:
            arrived[slots(me_w), my_cols] = outgoing[slots(me_w), :]

        def send(i, carry, q=q):
            send_copy(q * size + (inner + i) % size).start()
            return carry

        lax.fori_loop(1 if g == 0 else 0, size, send, 0)

    def forward_copy(g, q, m):
        part = arrived.at[group_rows(q), my_cols]
        return remote(part, part, xs.at[g, m], xr.at[g, me_n], (me_w, m))

    def forward_in(g, q, m):
        part = arrived.at[group_rows(q), cols(m)]
        return remote(part, part, xs.at[g, m], xr.at[g, m], (me_w, m))

    def partial_copy(g, q, m):
        return remote(
            partial.at[group_rows(q), cols(m)],
            partial_in.at[me_n, group_rows(q), :],
            ps.at[g, m],
            pr.at[g, me_n],
            (me_w, m),
        )

    def partial_wait(g, q, m):
        return remote(
            partial.at[group_rows(q), cols(m)],
            partial_in.at[m, group_rows(q), :],
            ps.at[g, m],
            pr.at[g, m],
            (me_w, m),
        )

    def return_copy(s):
        return remote(
            sums.at[slots(s), :],
            returned.at[slots(me_w), :],
            rs.at[s],
            rr.at[me_w],
            (s, me_n),
        )

    def return_wait(p):
        return remote(
            sums.at[slots(p), :],
            returned.at[slots(p), :],
            rs.at[p],
            rr.at[p],
            (p, me_n),
        )

    siblings = [(me_n + i) % narrow for i in range(1, narrow)]
    tile = min(512, units)

    def step(g, carry):
        q = plane_of(g)

        @pl.when(g == 1)
        def _():
            for load in loads[3:]:
                load.wait()

            def sort(i, c):
                r = pl.ds(pl.multiple_of(i * 64, 64), 64)
                pin[r, :channels] = pin_raw[r, 0, :]
                pin[r, channels:] = pin_raw[r, 1, :]
                return c

            lax.fori_loop(0, width // 64, sort, 0)

        def take(i, c):
            s = q * size + (inner + size - i) % size

            @pl.when(s != me_w)
            def _():
                recv_copy(s).wait_recv()

            return c

        lax.fori_loop(0, size, take, 0)
        for m in siblings:
            forward_copy(g, q, m).start()

        @pl.when(g == 0)
        def _():
            for load in loads[:3]:
                load.wait()

        for m in siblings:
            forward_in(g, q, m).wait_recv()

        x = arrived[group_rows(q), :]
        for f in range(0, units, tile):
            gate = jnp.dot(x, w_gate[:, f : f + tile], preferred_element_type=F32)
            up = jnp.dot(x, w_up[:, f : f + tile], preferred_element_type=F32)
            hidden[:, f : f + tile] = (gate * jax.nn.sigmoid(gate) * up).astype(BF16)
        for m in siblings:
            partial[group_rows(q), cols(m)] = jnp.dot(
                hidden[...], w_down[:, cols(m)], preferred_element_type=F32
            ).astype(BF16)
            partial_copy(g, q, m).start()
        total = jnp.dot(hidden[...], w_down[:, my_cols], preferred_element_type=F32)
        for m in siblings:
            partial_wait(g, q, m).wait_recv()
            total = total + partial_in[m, group_rows(q), :].astype(F32)
        sums[group_rows(q), :] = total.astype(BF16)

        def give(i, c):
            s = q * size + (inner + size - i) % size

            @pl.when(s != me_w)
            def _():
                return_copy(s).start()

            return c

        lax.fori_loop(0, size, give, 0)
        return carry

    lax.fori_loop(0, groups, step, 0)
    returned[slots(me_w), :] = sums[slots(me_w), :]

    mix0[...] = jnp.zeros_like(mix0)
    mix1[...] = jnp.zeros_like(mix1)

    def combine(g, carry):
        q = plane_of(g)

        def take(i, c):
            p = q * size + (inner + i) % size

            @pl.when(p != me_w)
            def _():
                return_wait(p).wait_recv()

            return c

        lax.fori_loop(0, size, take, 0)
        place = lax.broadcasted_iota(jnp.int32, (frame_count, rows), 1) + q * rows
        block = returned[group_rows(q), :]
        mix0[...] += jnp.dot(
            jnp.where(place == turned[:, 0:1].astype(jnp.int32), 1.0, 0.0).astype(BF16), block, preferred_element_type=F32
        )
        mix1[...] += jnp.dot(
            jnp.where(place == turned[:, 1:2].astype(jnp.int32), 1.0, 0.0).astype(BF16), block, preferred_element_type=F32
        )
        return carry

    lax.fori_loop(0, groups, combine, 0)
    mixed[:, my_cols] = (
        turned[:, 2:3] * mix0[...] + turned[:, 3:4] * mix1[...]
    ).astype(BF16)

    def mix_copy(m):
        part = mixed.at[:, my_cols]
        return remote(part, part, ms.at[m], mr.at[me_n], (me_w, m))

    def mix_wait(m):
        part = mixed.at[:, cols(m)]
        return remote(part, part, ms.at[m], mr.at[m], (me_w, m))

    for m in siblings:
        mix_copy(m).start()
    for m in siblings:
        mix_wait(m).wait_recv()

    res = frames_ref[...].astype(F32) + mixed[...].astype(F32)
    residual[...] = res
    centered = res - jnp.mean(res, axis=1, keepdims=True)
    variance = jnp.mean(centered * centered, axis=1, keepdims=True)
    normed = (centered * lax.rsqrt(variance + 1e-05) * gain_ref[...] + bias_ref[...]).astype(BF16)
    value_half = jnp.dot(normed, pin[:, :channels], preferred_element_type=F32)
    gate_half = jnp.dot(normed, pin[:, channels:], preferred_element_type=F32)
    glu = (value_half * jax.nn.sigmoid(gate_half)).astype(BF16)
    padded[HALO : HALO + frame_count, :] = glu
    padded32[HALO : HALO + frame_count, :] = glu.astype(F32)

    end = HALO + frame_count
    to_left = remote(
        padded.at[HALO : 2 * HALO, :],
        padded.at[end : end + HALO, :],
        hs.at[0],
        hr.at[0],
        ((me_w + wide - 1) % wide, me_n),
    )
    to_right = remote(
        padded.at[frame_count:end, :],
        padded.at[0:HALO, :],
        hs.at[1],
        hr.at[1],
        ((me_w + 1) % wide, me_n),
    )
    has_left = me_w > 0
    has_right = me_w < wide - 1

    @pl.when(has_left)
    def _():
        to_left.start()

    @pl.when(has_right)
    def _():
        to_right.start()

    half = (taps - 1) // 2
    step_rows = 64

    def depthwise(starts):
        def strip(c, carry):
            lanes = pl.ds(pl.multiple_of(c * 128, 128), 128)
            kernel_taps = depth_ref[:, lanes].astype(F32)
            for start in starts:
                total = jnp.zeros((step_rows, 128), F32)
                for j in range(taps):
                    low = start + HALO - half + j
                    total = total + padded32[low : low + step_rows, lanes] * kernel_taps[j : j + 1, :]
                activated[start : start + step_rows, lanes] = (
                    total * jax.nn.sigmoid(total)
                ).astype(BF16)
            return carry

        lax.fori_loop(0, channels // 128, strip, 0)

    depthwise(range(step_rows, frame_count - step_rows, step_rows))

    @pl.when(has_right)
    def _():
        to_left.wait_recv()
        padded32[end : end + HALO, :] = padded[end : end + HALO, :].astype(F32)

    @pl.when(jnp.logical_not(has_right))
    def _():
        padded32[end : end + HALO, :] = jnp.zeros((HALO, channels), F32)

    @pl.when(has_left)
    def _():
        to_right.wait_recv()
        padded32[0:HALO, :] = padded[0:HALO, :].astype(F32)

    @pl.when(jnp.logical_not(has_left))
    def _():
        padded32[0:HALO, :] = jnp.zeros((HALO, channels), F32)

    depthwise((0, frame_count - step_rows))

    def share_copy(m):
        return remote(
            shares.at[share_rows(m), :], shares_in.at[me_n], os_.at[m], or_.at[me_n], (me_w, m)
        )

    def share_wait(m):
        return remote(
            shares.at[share_rows(m), :], shares_in.at[m], os_.at[m], or_.at[m], (me_w, m)
        )

    for m in siblings:
        shares[share_rows(m), :] = jnp.dot(
            activated[share_rows(m), :], pout[...], preferred_element_type=F32
        ).astype(BF16)
        share_copy(m).start()
    total = residual[share_rows(me_n), :] + jnp.dot(
        activated[share_rows(me_n), :], pout[...], preferred_element_type=F32
    )
    for m in siblings:
        share_wait(m).wait_recv()
        total = total + shares_in[m].astype(F32)
    out_ref[...] = total.astype(BF16)

    def finish(i, carry):
        p = (me_w + i) % wide
        send_copy(p).wait_send()
        return_copy(p).wait_send()
        return carry

    lax.fori_loop(1, wide, finish, 0)
    for m in siblings:
        mix_copy(m).wait_send()
        share_copy(m).wait_send()

    def finish_group(g, carry):
        q = plane_of(g)
        for m in siblings:
            forward_copy(g, q, m).wait_send()
            partial_copy(g, q, m).wait_send()
        return carry

    lax.fori_loop(0, groups, finish_group, 0)

    @pl.when(has_left)
    def _():
        to_left.wait_send()

    @pl.when(has_right)
    def _():
        to_right.wait_send()


def shards(
    frames,
    expert_ids,
    gate_values,
    w_gate,
    w_up,
    w_down,
    norm_gain,
    norm_bias,
    point_in,
    depth_kernel,
    point_out,
):
    frame_count, width = frames.shape
    top_count = expert_ids.shape[1]
    wide = lax.axis_size("wide")
    narrow = lax.axis_size("narrow")
    expert_count = w_gate.shape[0] * wide
    cap = 2 * top_count * frame_count // expert_count
    units = w_gate.shape[2]
    channels = point_in.shape[2]
    groups = 4
    slot_count = wide * cap
    rows = slot_count // groups
    dc = width // narrow
    share = frame_count // narrow
    vmem = pl.BlockSpec(memory_space=pltpu.VMEM)
    hbm = pl.BlockSpec(memory_space=pl.ANY)
    dma = pltpu.SemaphoreType.DMA
    flops = 2 * width * (3 * slot_count * units + 3 * frame_count * channels)
    return pl.pallas_call(
        functools.partial(block_kernel, wide, narrow, groups, cap),
        out_shape=jax.ShapeDtypeStruct((share, width), BF16),
        in_specs=[vmem] * 6 + [hbm] * 5,
        out_specs=vmem,
        scratch_shapes=[
            pltpu.VMEM((width, units), BF16),
            pltpu.VMEM((width, units), BF16),
            pltpu.VMEM((units, width), BF16),
            pltpu.VMEM((width, 2, channels), BF16),
            pltpu.VMEM((width, 2 * channels), BF16),
            pltpu.VMEM((channels, width), BF16),
            pltpu.VMEM((frame_count, 128), F32),
            pltpu.VMEM((slot_count, dc), BF16),
            pltpu.VMEM((slot_count, width), BF16),
            pltpu.VMEM((rows, units), BF16),
            pltpu.VMEM((slot_count, width), BF16),
            pltpu.VMEM((narrow, slot_count, dc), BF16),
            pltpu.VMEM((slot_count, dc), BF16),
            pltpu.VMEM((slot_count, dc), BF16),
            pltpu.VMEM((frame_count, dc), F32),
            pltpu.VMEM((frame_count, dc), F32),
            pltpu.VMEM((frame_count, width), BF16),
            pltpu.VMEM((frame_count, width), F32),
            pltpu.VMEM((frame_count + 2 * HALO, channels), BF16),
            pltpu.VMEM((frame_count + 2 * HALO, channels), F32),
            pltpu.VMEM((frame_count, channels), BF16),
            pltpu.VMEM((frame_count, width), BF16),
            pltpu.VMEM((narrow, share, width), BF16),
            dma((5,)),
            dma((wide,)),
            dma((wide,)),
            dma((groups, narrow)),
            dma((groups, narrow)),
            dma((groups, narrow)),
            dma((groups, narrow)),
            dma((wide,)),
            dma((wide,)),
            dma((narrow,)),
            dma((narrow,)),
            dma((2,)),
            dma((2,)),
            dma((narrow,)),
            dma((narrow,)),
        ],
        compiler_params=pltpu.CompilerParams(
            collective_id=0, has_side_effects=True, vmem_limit_bytes=56 * 1024 * 1024
        ),
        cost_estimate=pl.CostEstimate(
            flops=flops, bytes_accessed=2 * 3 * width * units, transcendentals=0
        ),
        name="conformer_block",
    )(
        frames,
        expert_ids.T,
        gate_values.T,
        norm_gain.reshape(1, width),
        norm_bias.reshape(1, width),
        depth_kernel,
        w_gate,
        w_up,
        w_down,
        point_in,
        point_out,
    )


def solution(mesh):
    return jax.shard_map(
        shards,
        mesh=mesh,
        in_specs=(
            P("wide", None),
            P("wide", None),
            P("wide", None),
            P("wide", None, "narrow"),
            P("wide", None, "narrow"),
            P("wide", "narrow", None),
            P(),
            P(),
            P(None, None, "narrow"),
            P(None, "narrow"),
            P("narrow", None),
        ),
        out_specs=P(("wide", "narrow"), None),
        check_vma=False,
    )
```

```python
import functools

import jax
import jax.numpy as jnp
from jax import lax
from jax.experimental import pallas as pl
from jax.experimental.pallas import tpu as pltpu
from jax.sharding import PartitionSpec as P

F32 = jnp.float32
BF16 = jnp.bfloat16
HALO = 16


def block_kernel(
    wide,
    narrow,
    groups,
    cap,
    frames_ref,
    ids_ref,
    gates_ref,
    gain_ref,
    bias_ref,
    depth_ref,
    w_gate_hbm,
    w_up_hbm,
    w_down_hbm,
    pin_hbm,
    pout_hbm,
    out_ref,
    w_gate,
    w_up,
    w_down,
    pin_raw,
    pin,
    pout,
    turned,
    outgoing,
    arrived,
    hidden,
    partial,
    partial_in,
    sums,
    returned,
    mix0,
    mix1,
    mixed,
    residual,
    padded,
    padded32,
    activated,
    taps_all,
    w_sem,
    fs,
    fr,
    xs,
    xr,
    ps,
    pr,
    rs,
    rr,
    ms,
    mr,
    hs,
    hr,
    os_,
    or_,
    vs,
    vr,
    ts,
    tr,
):
    me_w = lax.axis_index("wide")
    me_n = lax.axis_index("narrow")
    frame_count, width = frames_ref.shape
    dc = width // narrow
    size = wide // groups
    rows = size * cap
    plane = me_w // size
    inner = me_w % size
    units = w_gate.shape[1]
    channels = pout.shape[0] // narrow
    share = frame_count // narrow
    taps = depth_ref.shape[0]
    total_count = wide * narrow
    place_now = me_w * narrow + me_n
    before = (place_now + total_count - 1) % total_count
    after = (place_now + 1) % total_count

    def cols(index):
        return pl.ds(pl.multiple_of(index * dc, 128), dc)

    def slots(index):
        return pl.ds(pl.multiple_of(index * cap, 16), cap)

    def group_rows(index):
        return pl.ds(pl.multiple_of(index * rows, 16), rows)

    def share_rows(index):
        return pl.ds(pl.multiple_of(index * share, 16), share)

    my_cols = cols(me_n)

    barrier = pltpu.get_barrier_semaphore()

    def greet(i, carry):
        pl.semaphore_signal(
            barrier,
            inc=1,
            device_id=((me_w + i) % wide, me_n),
            device_id_type=pl.DeviceIdType.MESH,
        )
        return carry

    lax.fori_loop(1, wide, greet, 0)
    for i in range(1, narrow):
        pl.semaphore_signal(
            barrier,
            inc=1,
            device_id=(me_w, (me_n + i) % narrow),
            device_id_type=pl.DeviceIdType.MESH,
        )

    for other in (before, after):
        pl.semaphore_signal(
            barrier,
            inc=1,
            device_id=(other // narrow, other % narrow),
            device_id_type=pl.DeviceIdType.MESH,
        )

    own_channels = pl.ds(pl.multiple_of(me_n * channels, 128), channels)

    loads = [
        pltpu.make_async_copy(w_gate_hbm.at[0], w_gate, w_sem.at[0]),
        pltpu.make_async_copy(w_up_hbm.at[0], w_up, w_sem.at[1]),
        pltpu.make_async_copy(w_down_hbm.at[0], w_down, w_sem.at[2]),
        pltpu.make_async_copy(pin_hbm, pin_raw, w_sem.at[3]),
        pltpu.make_async_copy(pout_hbm, pout.at[own_channels, :], w_sem.at[4]),
    ]
    for load in loads:
        load.start()

    def remote(src, dst, send, recv, device):
        return pltpu.make_async_remote_copy(
            src_ref=src,
            dst_ref=dst,
            send_sem=send,
            recv_sem=recv,
            device_id=device,
            device_id_type=pl.DeviceIdType.MESH,
        )

    id0 = ids_ref[0:1, :]
    id1 = ids_ref[1:2, :]
    lane = lax.broadcasted_iota(jnp.int32, (128, frame_count), 0)
    named0 = lane == id0
    named1 = lane == id1
    named = jnp.where(named0 | named1, 1.0, 0.0).astype(BF16)
    earlier = jnp.where(
        lax.broadcasted_iota(jnp.int32, (frame_count, frame_count), 0)
        < lax.broadcasted_iota(jnp.int32, (frame_count, frame_count), 1),
        1.0,
        0.0,
    ).astype(BF16)
    position = jnp.dot(named, earlier, preferred_element_type=F32)
    row0 = id0.astype(F32) * cap + jnp.sum(
        jnp.where(named0, position, 0.0), axis=0, keepdims=True
    )
    row1 = id1.astype(F32) * cap + jnp.sum(
        jnp.where(named1, position, 0.0), axis=0, keepdims=True
    )
    stacked = jnp.where(
        lane == 0,
        row0,
        jnp.where(
            lane == 1, row1, jnp.where(lane == 2, gates_ref[0:1, :], gates_ref[1:2, :])
        ),
    )
    turned[...] = jnp.transpose(stacked)
    row0 = row0.astype(jnp.int32)
    row1 = row1.astype(jnp.int32)

    def plane_of(g):
        return ((plane // 2 + g % 2) % 2) * 2 + (plane % 2 + g // 2) % 2

    def send_copy(p):
        return remote(
            outgoing.at[slots(p), :],
            arrived.at[slots(me_w), my_cols],
            fs.at[p],
            fr.at[me_w],
            (p, me_n),
        )

    def recv_copy(s):
        return remote(
            outgoing.at[slots(s), :],
            arrived.at[slots(s), my_cols],
            fs.at[s],
            fr.at[s],
            (s, me_n),
        )

    mine = frames_ref[:, my_cols]
    for turn, g in enumerate((1, 0, 3, 2)):
        q = plane_of(g)
        place = lax.broadcasted_iota(jnp.int32, (rows, frame_count), 0) + q * rows
        choose = jnp.where((place == row0) | (place == row1), 1.0, 0.0).astype(BF16)
        outgoing[group_rows(q), :] = jnp.dot(
            choose, mine, preferred_element_type=F32
        ).astype(BF16)
        if turn == 0:
            pl.semaphore_wait(barrier, wide - 1 + narrow - 1 + 2)
        if g == 0:
            arrived[slots(me_w), my_cols] = outgoing[slots(me_w), :]

        def send(i, carry, q=q):
            send_copy(q * size + (inner + i) % size).start()
            return carry

        lax.fori_loop(1 if g == 0 else 0, size, send, 0)

    def forward_copy(g, q, m):
        part = arrived.at[group_rows(q), my_cols]
        return remote(part, part, xs.at[g, m], xr.at[g, me_n], (me_w, m))

    def forward_in(g, q, m):
        part = arrived.at[group_rows(q), cols(m)]
        return remote(part, part, xs.at[g, m], xr.at[g, m], (me_w, m))

    def partial_copy(g, q, m):
        return remote(
            partial.at[group_rows(q), cols(m)],
            partial_in.at[me_n, group_rows(q), :],
            ps.at[g, m],
            pr.at[g, me_n],
            (me_w, m),
        )

    def partial_wait(g, q, m):
        return remote(
            partial.at[group_rows(q), cols(m)],
            partial_in.at[m, group_rows(q), :],
            ps.at[g, m],
            pr.at[g, m],
            (me_w, m),
        )

    def return_copy(s):
        return remote(
            sums.at[slots(s), :],
            returned.at[slots(me_w), :],
            rs.at[s],
            rr.at[me_w],
            (s, me_n),
        )

    def return_wait(p):
        return remote(
            sums.at[slots(p), :],
            returned.at[slots(p), :],
            rs.at[p],
            rr.at[p],
            (p, me_n),
        )

    def weight_copies(m):
        taps_part = taps_all.at[me_n]
        pin_part = pin.at[me_n]
        pout_part = pout.at[own_channels, :]
        return (
            remote(taps_part, taps_part, ts.at[m], tr.at[me_n], (me_w, m)),
            remote(pin_part, pin_part, vs.at[m], vr.at[me_n], (me_w, m)),
            remote(pout_part, pout_part, os_.at[m], or_.at[me_n], (me_w, m)),
        )

    def weight_waits(m):
        taps_part = taps_all.at[m]
        pin_part = pin.at[m]
        pout_part = pout.at[pl.ds(pl.multiple_of(m * channels, 128), channels), :]
        return (
            remote(taps_part, taps_part, ts.at[m], tr.at[m], (me_w, m)),
            remote(pin_part, pin_part, vs.at[m], vr.at[m], (me_w, m)),
            remote(pout_part, pout_part, os_.at[m], or_.at[m], (me_w, m)),
        )

    siblings = [(me_n + i) % narrow for i in range(1, narrow)]
    tile = min(512, units)

    def step(g, carry):
        q = plane_of(g)

        @pl.when(g == 1)
        def _():
            for load in loads[3:]:
                load.wait()

            def sort(i, c):
                r = pl.ds(pl.multiple_of(i * 64, 64), 64)
                pin[me_n, r, :channels] = pin_raw[r, 0, :]
                pin[me_n, r, channels:] = pin_raw[r, 1, :]
                return c

            lax.fori_loop(0, width // 64, sort, 0)
            taps_all[me_n] = jnp.zeros(taps_all.shape[1:], F32)
            taps_all[me_n, 0:taps, :] = depth_ref[...].astype(F32)
            for m in siblings:
                for copy in weight_copies(m):
                    copy.start()

        def take(i, c):
            s = q * size + (inner + size - i) % size

            @pl.when(s != me_w)
            def _():
                recv_copy(s).wait_recv()

            return c

        lax.fori_loop(0, size, take, 0)
        for m in siblings:
            forward_copy(g, q, m).start()

        @pl.when(g == 0)
        def _():
            for load in loads[:3]:
                load.wait()

        for m in siblings:
            forward_in(g, q, m).wait_recv()

        x = arrived[group_rows(q), :]
        for f in range(0, units, tile):
            gate = jnp.dot(x, w_gate[:, f : f + tile], preferred_element_type=F32)
            up = jnp.dot(x, w_up[:, f : f + tile], preferred_element_type=F32)
            hidden[:, f : f + tile] = (gate * jax.nn.sigmoid(gate) * up).astype(BF16)
        for m in siblings:
            partial[group_rows(q), cols(m)] = jnp.dot(
                hidden[...], w_down[:, cols(m)], preferred_element_type=F32
            ).astype(BF16)
            partial_copy(g, q, m).start()
        total = jnp.dot(hidden[...], w_down[:, my_cols], preferred_element_type=F32)
        for m in siblings:
            partial_wait(g, q, m).wait_recv()
            total = total + partial_in[m, group_rows(q), :].astype(F32)
        sums[group_rows(q), :] = total.astype(BF16)

        def give(i, c):
            s = q * size + (inner + size - i) % size

            @pl.when(s != me_w)
            def _():
                return_copy(s).start()

            return c

        lax.fori_loop(0, size, give, 0)
        return carry

    lax.fori_loop(0, groups, step, 0)
    returned[slots(me_w), :] = sums[slots(me_w), :]

    mix0[...] = jnp.zeros_like(mix0)
    mix1[...] = jnp.zeros_like(mix1)

    def combine(g, carry):
        q = plane_of(g)

        def take(i, c):
            p = q * size + (inner + i) % size

            @pl.when(p != me_w)
            def _():
                return_wait(p).wait_recv()

            return c

        lax.fori_loop(0, size, take, 0)
        place = lax.broadcasted_iota(jnp.int32, (frame_count, rows), 1) + q * rows
        block = returned[group_rows(q), :]
        mix0[...] += jnp.dot(
            jnp.where(place == turned[:, 0:1].astype(jnp.int32), 1.0, 0.0).astype(BF16), block, preferred_element_type=F32
        )
        mix1[...] += jnp.dot(
            jnp.where(place == turned[:, 1:2].astype(jnp.int32), 1.0, 0.0).astype(BF16), block, preferred_element_type=F32
        )
        return carry

    lax.fori_loop(0, groups, combine, 0)
    mixed[:, my_cols] = (
        turned[:, 2:3] * mix0[...] + turned[:, 3:4] * mix1[...]
    ).astype(BF16)

    own_rows = share_rows(me_n)

    def mix_copy(m):
        part = mixed.at[share_rows(m), my_cols]
        return remote(part, part, ms.at[m], mr.at[me_n], (me_w, m))

    def mix_wait(m):
        part = mixed.at[own_rows, cols(m)]
        return remote(part, part, ms.at[m], mr.at[m], (me_w, m))

    for m in siblings:
        mix_copy(m).start()
    for m in siblings:
        for copy in weight_waits(m):
            copy.wait_recv()
    for m in siblings:
        mix_wait(m).wait_recv()

    res = frames_ref[own_rows, :].astype(F32) + mixed[own_rows, :].astype(F32)
    residual[...] = res
    centered = res - jnp.mean(res, axis=1, keepdims=True)
    variance = jnp.mean(centered * centered, axis=1, keepdims=True)
    normed = (centered * lax.rsqrt(variance + 1e-05) * gain_ref[...] + bias_ref[...]).astype(BF16)
    end = HALO + share
    for m in range(narrow):
        value_half = jnp.dot(normed, pin[m, :, :channels], preferred_element_type=F32)
        gate_half = jnp.dot(normed, pin[m, :, channels:], preferred_element_type=F32)
        glu = (value_half * jax.nn.sigmoid(gate_half)).astype(BF16)
        padded[HALO:end, m * channels : (m + 1) * channels] = glu
        padded32[HALO:end, m * channels : (m + 1) * channels] = glu.astype(F32)

    to_left = remote(
        padded.at[HALO : 2 * HALO, :],
        padded.at[end : end + HALO, :],
        hs.at[0],
        hr.at[0],
        (before // narrow, before % narrow),
    )
    to_right = remote(
        padded.at[share:end, :],
        padded.at[0:HALO, :],
        hs.at[1],
        hr.at[1],
        (after // narrow, after % narrow),
    )
    has_left = place_now > 0
    has_right = place_now < total_count - 1

    @pl.when(has_left)
    def _():
        to_left.start()

    @pl.when(has_right)
    def _():
        to_right.start()

    half = (taps - 1) // 2
    step_rows = min(32, share)

    def depthwise(starts):
        for m in range(narrow):

            def strip(c, carry, m=m):
                lanes = pl.ds(pl.multiple_of(m * channels + c * 128, 128), 128)
                kernel_taps = taps_all[m, :, pl.ds(pl.multiple_of(c * 128, 128), 128)]
                for start in starts:
                    total = jnp.zeros((step_rows, 128), F32)
                    for j in range(taps):
                        low = start + HALO - half + j
                        total = (
                            total
                            + padded32[low : low + step_rows, lanes] * kernel_taps[j : j + 1, :]
                        )
                    activated[start : start + step_rows, lanes] = (
                        total * jax.nn.sigmoid(total)
                    ).astype(BF16)
                return carry

            lax.fori_loop(0, channels // 128, strip, 0)

    edges = sorted({0, share - step_rows})
    inside = [start for start in range(0, share, step_rows) if start not in edges]
    if inside:
        depthwise(inside)

    @pl.when(has_right)
    def _():
        to_left.wait_recv()
        padded32[end : end + HALO, :] = padded[end : end + HALO, :].astype(F32)

    @pl.when(jnp.logical_not(has_right))
    def _():
        padded32[end : end + HALO, :] = jnp.zeros((HALO, width), F32)

    @pl.when(has_left)
    def _():
        to_right.wait_recv()
        padded32[0:HALO, :] = padded[0:HALO, :].astype(F32)

    @pl.when(jnp.logical_not(has_left))
    def _():
        padded32[0:HALO, :] = jnp.zeros((HALO, width), F32)

    depthwise(edges)

    out_ref[...] = (
        residual[...] + jnp.dot(activated[...], pout[...], preferred_element_type=F32)
    ).astype(BF16)

    def finish(i, carry):
        p = (me_w + i) % wide
        send_copy(p).wait_send()
        return_copy(p).wait_send()
        return carry

    lax.fori_loop(1, wide, finish, 0)
    for m in siblings:
        mix_copy(m).wait_send()
        for copy in weight_copies(m):
            copy.wait_send()

    def finish_group(g, carry):
        q = plane_of(g)
        for m in siblings:
            forward_copy(g, q, m).wait_send()
            partial_copy(g, q, m).wait_send()
        return carry

    lax.fori_loop(0, groups, finish_group, 0)

    @pl.when(has_left)
    def _():
        to_left.wait_send()

    @pl.when(has_right)
    def _():
        to_right.wait_send()


def shards(
    frames,
    expert_ids,
    gate_values,
    w_gate,
    w_up,
    w_down,
    norm_gain,
    norm_bias,
    point_in,
    depth_kernel,
    point_out,
):
    frame_count, width = frames.shape
    top_count = expert_ids.shape[1]
    wide = lax.axis_size("wide")
    narrow = lax.axis_size("narrow")
    expert_count = w_gate.shape[0] * wide
    cap = 2 * top_count * frame_count // expert_count
    units = w_gate.shape[2]
    channels = point_in.shape[2]
    groups = 4
    slot_count = wide * cap
    rows = slot_count // groups
    dc = width // narrow
    share = frame_count // narrow
    vmem = pl.BlockSpec(memory_space=pltpu.VMEM)
    hbm = pl.BlockSpec(memory_space=pl.ANY)
    dma = pltpu.SemaphoreType.DMA
    flops = 2 * width * (3 * slot_count * units + 3 * frame_count * channels)
    return pl.pallas_call(
        functools.partial(block_kernel, wide, narrow, groups, cap),
        out_shape=jax.ShapeDtypeStruct((share, width), BF16),
        in_specs=[vmem] * 6 + [hbm] * 5,
        out_specs=vmem,
        scratch_shapes=[
            pltpu.VMEM((width, units), BF16),
            pltpu.VMEM((width, units), BF16),
            pltpu.VMEM((units, width), BF16),
            pltpu.VMEM((width, 2, channels), BF16),
            pltpu.VMEM((narrow, width, 2 * channels), BF16),
            pltpu.VMEM((narrow * channels, width), BF16),
            pltpu.VMEM((frame_count, 128), F32),
            pltpu.VMEM((slot_count, dc), BF16),
            pltpu.VMEM((slot_count, width), BF16),
            pltpu.VMEM((rows, units), BF16),
            pltpu.VMEM((slot_count, width), BF16),
            pltpu.VMEM((narrow, slot_count, dc), BF16),
            pltpu.VMEM((slot_count, dc), BF16),
            pltpu.VMEM((slot_count, dc), BF16),
            pltpu.VMEM((frame_count, dc), F32),
            pltpu.VMEM((frame_count, dc), F32),
            pltpu.VMEM((frame_count, width), BF16),
            pltpu.VMEM((share, width), F32),
            pltpu.VMEM((share + 2 * HALO, narrow * channels), BF16),
            pltpu.VMEM((share + 2 * HALO, narrow * channels), F32),
            pltpu.VMEM((share, narrow * channels), BF16),
            pltpu.VMEM((narrow, -(-depth_kernel.shape[0] // 8) * 8, channels), F32),
            dma((5,)),
            dma((wide,)),
            dma((wide,)),
            dma((groups, narrow)),
            dma((groups, narrow)),
            dma((groups, narrow)),
            dma((groups, narrow)),
            dma((wide,)),
            dma((wide,)),
            dma((narrow,)),
            dma((narrow,)),
            dma((2,)),
            dma((2,)),
            dma((narrow,)),
            dma((narrow,)),
            dma((narrow,)),
            dma((narrow,)),
            dma((narrow,)),
            dma((narrow,)),
        ],
        compiler_params=pltpu.CompilerParams(
            collective_id=0, has_side_effects=True, vmem_limit_bytes=56 * 1024 * 1024
        ),
        cost_estimate=pl.CostEstimate(
            flops=flops, bytes_accessed=2 * 3 * width * units, transcendentals=0
        ),
        name="conformer_block",
    )(
        frames,
        expert_ids.T,
        gate_values.T,
        norm_gain.reshape(1, width),
        norm_bias.reshape(1, width),
        depth_kernel,
        w_gate,
        w_up,
        w_down,
        point_in,
        point_out,
    )


def solution(mesh):
    return jax.shard_map(
        shards,
        mesh=mesh,
        in_specs=(
            P("wide", None),
            P("wide", None),
            P("wide", None),
            P("wide", None, "narrow"),
            P("wide", None, "narrow"),
            P("wide", "narrow", None),
            P(),
            P(),
            P(None, None, "narrow"),
            P(None, "narrow"),
            P("narrow", None),
        ),
        out_specs=P(("wide", "narrow"), None),
        check_vma=False,
    )
```

```python
import functools

import jax
import jax.numpy as jnp
from jax import lax
from jax.experimental import pallas as pl
from jax.experimental.pallas import tpu as pltpu
from jax.sharding import PartitionSpec as P

F32 = jnp.float32
BF16 = jnp.bfloat16
HALO = 16


def block_kernel(
    wide,
    narrow,
    groups,
    cap,
    frames_ref,
    ids_ref,
    gates_ref,
    gain_ref,
    bias_ref,
    depth_ref,
    w_gate_hbm,
    w_up_hbm,
    w_down_hbm,
    pin_hbm,
    pout_hbm,
    out_ref,
    w_gate,
    w_up,
    w_down,
    pin_raw,
    pin,
    pout,
    turned,
    outgoing,
    arrived,
    hidden,
    partial,
    partial_in,
    sums,
    returned,
    mix0,
    mix1,
    mixed,
    residual,
    padded,
    padded32,
    activated,
    taps_all,
    w_sem,
    fs,
    fr,
    xs,
    xr,
    ps,
    pr,
    rs,
    rr,
    ms,
    mr,
    hs,
    hr,
    os_,
    or_,
    vs,
    vr,
    ts,
    tr,
):
    me_w = lax.axis_index("wide")
    me_n = lax.axis_index("narrow")
    frame_count, width = frames_ref.shape
    dc = width // narrow
    size = wide // groups
    rows = size * cap
    plane = me_w // size
    inner = me_w % size
    units = w_gate.shape[1]
    channels = pout.shape[0] // narrow
    share = frame_count // narrow
    taps = depth_ref.shape[0]
    total_count = wide * narrow
    place_now = me_w * narrow + me_n
    before = (place_now + total_count - 1) % total_count
    after = (place_now + 1) % total_count

    def cols(index):
        return pl.ds(pl.multiple_of(index * dc, 128), dc)

    def slots(index):
        return pl.ds(pl.multiple_of(index * cap, 16), cap)

    def group_rows(index):
        return pl.ds(pl.multiple_of(index * rows, 16), rows)

    def share_rows(index):
        return pl.ds(pl.multiple_of(index * share, 16), share)

    my_cols = cols(me_n)

    barrier = pltpu.get_barrier_semaphore()

    def greet(i, carry):
        pl.semaphore_signal(
            barrier,
            inc=1,
            device_id=((me_w + i) % wide, me_n),
            device_id_type=pl.DeviceIdType.MESH,
        )
        return carry

    lax.fori_loop(1, wide, greet, 0)
    for i in range(1, narrow):
        pl.semaphore_signal(
            barrier,
            inc=1,
            device_id=(me_w, (me_n + i) % narrow),
            device_id_type=pl.DeviceIdType.MESH,
        )

    for other in (before, after):
        pl.semaphore_signal(
            barrier,
            inc=1,
            device_id=(other // narrow, other % narrow),
            device_id_type=pl.DeviceIdType.MESH,
        )

    own_channels = pl.ds(pl.multiple_of(me_n * channels, 128), channels)

    loads = [
        pltpu.make_async_copy(w_gate_hbm.at[0], w_gate, w_sem.at[0]),
        pltpu.make_async_copy(w_up_hbm.at[0], w_up, w_sem.at[1]),
        pltpu.make_async_copy(w_down_hbm.at[0], w_down, w_sem.at[2]),
        pltpu.make_async_copy(pin_hbm, pin_raw, w_sem.at[3]),
        pltpu.make_async_copy(pout_hbm, pout.at[own_channels, :], w_sem.at[4]),
    ]
    for load in loads:
        load.start()

    def remote(src, dst, send, recv, device):
        return pltpu.make_async_remote_copy(
            src_ref=src,
            dst_ref=dst,
            send_sem=send,
            recv_sem=recv,
            device_id=device,
            device_id_type=pl.DeviceIdType.MESH,
        )

    id0 = ids_ref[0:1, :]
    id1 = ids_ref[1:2, :]
    lane = lax.broadcasted_iota(jnp.int32, (128, frame_count), 0)
    named0 = lane == id0
    named1 = lane == id1
    named = jnp.where(named0 | named1, 1.0, 0.0).astype(BF16)
    earlier = jnp.where(
        lax.broadcasted_iota(jnp.int32, (frame_count, frame_count), 0)
        < lax.broadcasted_iota(jnp.int32, (frame_count, frame_count), 1),
        1.0,
        0.0,
    ).astype(BF16)
    position = jnp.dot(named, earlier, preferred_element_type=F32)
    row0 = id0.astype(F32) * cap + jnp.sum(
        jnp.where(named0, position, 0.0), axis=0, keepdims=True
    )
    row1 = id1.astype(F32) * cap + jnp.sum(
        jnp.where(named1, position, 0.0), axis=0, keepdims=True
    )
    stacked = jnp.where(
        lane == 0,
        row0,
        jnp.where(
            lane == 1, row1, jnp.where(lane == 2, gates_ref[0:1, :], gates_ref[1:2, :])
        ),
    )
    turned[...] = jnp.transpose(stacked)
    row0 = row0.astype(jnp.int32)
    row1 = row1.astype(jnp.int32)

    def plane_of(g):
        return ((plane // 2 + g % 2) % 2) * 2 + (plane % 2 + g // 2) % 2

    def send_copy(p):
        return remote(
            outgoing.at[slots(p), :],
            arrived.at[slots(me_w), my_cols],
            fs.at[p],
            fr.at[me_w],
            (p, me_n),
        )

    def recv_copy(s):
        return remote(
            outgoing.at[slots(s), :],
            arrived.at[slots(s), my_cols],
            fs.at[s],
            fr.at[s],
            (s, me_n),
        )

    mine = frames_ref[:, my_cols]
    for turn, g in enumerate((1, 0, 3, 2)):
        q = plane_of(g)
        place = lax.broadcasted_iota(jnp.int32, (rows, frame_count), 0) + q * rows
        choose = jnp.where((place == row0) | (place == row1), 1.0, 0.0).astype(BF16)
        outgoing[group_rows(q), :] = jnp.dot(
            choose, mine, preferred_element_type=F32
        ).astype(BF16)
        if turn == 0:
            pl.semaphore_wait(barrier, wide - 1 + narrow - 1 + 2)
        if g == 0:
            arrived[slots(me_w), my_cols] = outgoing[slots(me_w), :]

        def send(i, carry, q=q):
            send_copy(q * size + (inner + i) % size).start()
            return carry

        lax.fori_loop(1 if g == 0 else 0, size, send, 0)

    def forward_copy(g, q, m):
        part = arrived.at[group_rows(q), my_cols]
        return remote(part, part, xs.at[g, m], xr.at[g, me_n], (me_w, m))

    def forward_in(g, q, m):
        part = arrived.at[group_rows(q), cols(m)]
        return remote(part, part, xs.at[g, m], xr.at[g, m], (me_w, m))

    def partial_copy(g, q, m):
        return remote(
            partial.at[group_rows(q), cols(m)],
            partial_in.at[me_n, group_rows(q), :],
            ps.at[g, m],
            pr.at[g, me_n],
            (me_w, m),
        )

    def partial_wait(g, q, m):
        return remote(
            partial.at[group_rows(q), cols(m)],
            partial_in.at[m, group_rows(q), :],
            ps.at[g, m],
            pr.at[g, m],
            (me_w, m),
        )

    def return_copy(s):
        return remote(
            sums.at[slots(s), :],
            returned.at[slots(me_w), :],
            rs.at[s],
            rr.at[me_w],
            (s, me_n),
        )

    def return_wait(p):
        return remote(
            sums.at[slots(p), :],
            returned.at[slots(p), :],
            rs.at[p],
            rr.at[p],
            (p, me_n),
        )

    def weight_copies(m):
        taps_part = taps_all.at[me_n]
        pin_part = pin.at[me_n]
        pout_part = pout.at[own_channels, :]
        return (
            remote(taps_part, taps_part, ts.at[m], tr.at[me_n], (me_w, m)),
            remote(pin_part, pin_part, vs.at[m], vr.at[me_n], (me_w, m)),
            remote(pout_part, pout_part, os_.at[m], or_.at[me_n], (me_w, m)),
        )

    def weight_waits(m):
        taps_part = taps_all.at[m]
        pin_part = pin.at[m]
        pout_part = pout.at[pl.ds(pl.multiple_of(m * channels, 128), channels), :]
        return (
            remote(taps_part, taps_part, ts.at[m], tr.at[m], (me_w, m)),
            remote(pin_part, pin_part, vs.at[m], vr.at[m], (me_w, m)),
            remote(pout_part, pout_part, os_.at[m], or_.at[m], (me_w, m)),
        )

    siblings = [(me_n + i) % narrow for i in range(1, narrow)]
    tile = min(512, units)

    def step(g, carry):
        q = plane_of(g)

        @pl.when(g == groups - 1)
        def _():
            for load in loads[3:]:
                load.wait()

            def sort(i, c):
                r = pl.ds(pl.multiple_of(i * 64, 64), 64)
                pin[me_n, r, :channels] = pin_raw[r, 0, :]
                pin[me_n, r, channels:] = pin_raw[r, 1, :]
                return c

            lax.fori_loop(0, width // 64, sort, 0)
            taps_all[me_n] = jnp.zeros(taps_all.shape[1:], F32)
            taps_all[me_n, 0:taps, :] = depth_ref[...].astype(F32)

        def take(i, c):
            s = q * size + (inner + size - i) % size

            @pl.when(s != me_w)
            def _():
                recv_copy(s).wait_recv()

            return c

        lax.fori_loop(0, size, take, 0)
        for m in siblings:
            forward_copy(g, q, m).start()

        @pl.when(g == 0)
        def _():
            for load in loads[:3]:
                load.wait()

        for m in siblings:
            forward_in(g, q, m).wait_recv()

        x = arrived[group_rows(q), :]
        for f in range(0, units, tile):
            gate = jnp.dot(x, w_gate[:, f : f + tile], preferred_element_type=F32)
            up = jnp.dot(x, w_up[:, f : f + tile], preferred_element_type=F32)
            hidden[:, f : f + tile] = (gate * jax.nn.sigmoid(gate) * up).astype(BF16)
        for m in siblings:
            partial[group_rows(q), cols(m)] = jnp.dot(
                hidden[...], w_down[:, cols(m)], preferred_element_type=F32
            ).astype(BF16)
            partial_copy(g, q, m).start()
        total = jnp.dot(hidden[...], w_down[:, my_cols], preferred_element_type=F32)
        for m in siblings:
            partial_wait(g, q, m).wait_recv()
            total = total + partial_in[m, group_rows(q), :].astype(F32)
        sums[group_rows(q), :] = total.astype(BF16)

        def give(i, c):
            s = q * size + (inner + size - i) % size

            @pl.when(s != me_w)
            def _():
                return_copy(s).start()

            return c

        lax.fori_loop(0, size, give, 0)
        return carry

    lax.fori_loop(0, groups, step, 0)
    for m in siblings:
        for copy in weight_copies(m):
            copy.start()
    returned[slots(me_w), :] = sums[slots(me_w), :]

    mix0[...] = jnp.zeros_like(mix0)
    mix1[...] = jnp.zeros_like(mix1)

    def combine(g, carry):
        q = plane_of(g)

        def take(i, c):
            p = q * size + (inner + i) % size

            @pl.when(p != me_w)
            def _():
                return_wait(p).wait_recv()

            return c

        lax.fori_loop(0, size, take, 0)
        place = lax.broadcasted_iota(jnp.int32, (frame_count, rows), 1) + q * rows
        block = returned[group_rows(q), :]
        mix0[...] += jnp.dot(
            jnp.where(place == turned[:, 0:1].astype(jnp.int32), 1.0, 0.0).astype(BF16), block, preferred_element_type=F32
        )
        mix1[...] += jnp.dot(
            jnp.where(place == turned[:, 1:2].astype(jnp.int32), 1.0, 0.0).astype(BF16), block, preferred_element_type=F32
        )
        return carry

    lax.fori_loop(0, groups, combine, 0)
    mixed[:, my_cols] = (
        turned[:, 2:3] * mix0[...] + turned[:, 3:4] * mix1[...]
    ).astype(BF16)

    own_rows = share_rows(me_n)

    def mix_copy(m):
        part = mixed.at[share_rows(m), my_cols]
        return remote(part, part, ms.at[m], mr.at[me_n], (me_w, m))

    def mix_wait(m):
        part = mixed.at[own_rows, cols(m)]
        return remote(part, part, ms.at[m], mr.at[m], (me_w, m))

    for m in siblings:
        mix_copy(m).start()
    for m in siblings:
        for copy in weight_waits(m):
            copy.wait_recv()
    for m in siblings:
        mix_wait(m).wait_recv()

    res = frames_ref[own_rows, :].astype(F32) + mixed[own_rows, :].astype(F32)
    residual[...] = res
    centered = res - jnp.mean(res, axis=1, keepdims=True)
    variance = jnp.mean(centered * centered, axis=1, keepdims=True)
    normed = (centered * lax.rsqrt(variance + 1e-05) * gain_ref[...] + bias_ref[...]).astype(BF16)
    end = HALO + share
    for m in range(narrow):
        value_half = jnp.dot(normed, pin[m, :, :channels], preferred_element_type=F32)
        gate_half = jnp.dot(normed, pin[m, :, channels:], preferred_element_type=F32)
        glu = (value_half * jax.nn.sigmoid(gate_half)).astype(BF16)
        padded[HALO:end, m * channels : (m + 1) * channels] = glu
        padded32[HALO:end, m * channels : (m + 1) * channels] = glu.astype(F32)

    to_left = remote(
        padded.at[HALO : 2 * HALO, :],
        padded.at[end : end + HALO, :],
        hs.at[0],
        hr.at[0],
        (before // narrow, before % narrow),
    )
    to_right = remote(
        padded.at[share:end, :],
        padded.at[0:HALO, :],
        hs.at[1],
        hr.at[1],
        (after // narrow, after % narrow),
    )
    has_left = place_now > 0
    has_right = place_now < total_count - 1

    @pl.when(has_left)
    def _():
        to_left.start()

    @pl.when(has_right)
    def _():
        to_right.start()

    half = (taps - 1) // 2
    step_rows = min(32, share)

    def depthwise(starts):
        for m in range(narrow):

            def strip(c, carry, m=m):
                lanes = pl.ds(pl.multiple_of(m * channels + c * 128, 128), 128)
                kernel_taps = taps_all[m, :, pl.ds(pl.multiple_of(c * 128, 128), 128)]
                for start in starts:
                    total = jnp.zeros((step_rows, 128), F32)
                    for j in range(taps):
                        low = start + HALO - half + j
                        total = (
                            total
                            + padded32[low : low + step_rows, lanes] * kernel_taps[j : j + 1, :]
                        )
                    activated[start : start + step_rows, lanes] = (
                        total * jax.nn.sigmoid(total)
                    ).astype(BF16)
                return carry

            lax.fori_loop(0, channels // 128, strip, 0)

    edges = sorted({0, share - step_rows})
    inside = [start for start in range(0, share, step_rows) if start not in edges]
    if inside:
        depthwise(inside)

    @pl.when(has_right)
    def _():
        to_left.wait_recv()
        padded32[end : end + HALO, :] = padded[end : end + HALO, :].astype(F32)

    @pl.when(jnp.logical_not(has_right))
    def _():
        padded32[end : end + HALO, :] = jnp.zeros((HALO, width), F32)

    @pl.when(has_left)
    def _():
        to_right.wait_recv()
        padded32[0:HALO, :] = padded[0:HALO, :].astype(F32)

    @pl.when(jnp.logical_not(has_left))
    def _():
        padded32[0:HALO, :] = jnp.zeros((HALO, width), F32)

    depthwise(edges)

    out_ref[...] = (
        residual[...] + jnp.dot(activated[...], pout[...], preferred_element_type=F32)
    ).astype(BF16)

    def finish(i, carry):
        p = (me_w + i) % wide
        send_copy(p).wait_send()
        return_copy(p).wait_send()
        return carry

    lax.fori_loop(1, wide, finish, 0)
    for m in siblings:
        mix_copy(m).wait_send()
        for copy in weight_copies(m):
            copy.wait_send()

    def finish_group(g, carry):
        q = plane_of(g)
        for m in siblings:
            forward_copy(g, q, m).wait_send()
            partial_copy(g, q, m).wait_send()
        return carry

    lax.fori_loop(0, groups, finish_group, 0)

    @pl.when(has_left)
    def _():
        to_left.wait_send()

    @pl.when(has_right)
    def _():
        to_right.wait_send()


def shards(
    frames,
    expert_ids,
    gate_values,
    w_gate,
    w_up,
    w_down,
    norm_gain,
    norm_bias,
    point_in,
    depth_kernel,
    point_out,
):
    frame_count, width = frames.shape
    top_count = expert_ids.shape[1]
    wide = lax.axis_size("wide")
    narrow = lax.axis_size("narrow")
    expert_count = w_gate.shape[0] * wide
    cap = 2 * top_count * frame_count // expert_count
    units = w_gate.shape[2]
    channels = point_in.shape[2]
    groups = 4
    slot_count = wide * cap
    rows = slot_count // groups
    dc = width // narrow
    share = frame_count // narrow
    vmem = pl.BlockSpec(memory_space=pltpu.VMEM)
    hbm = pl.BlockSpec(memory_space=pl.ANY)
    dma = pltpu.SemaphoreType.DMA
    flops = 2 * width * (3 * slot_count * units + 3 * frame_count * channels)
    return pl.pallas_call(
        functools.partial(block_kernel, wide, narrow, groups, cap),
        out_shape=jax.ShapeDtypeStruct((share, width), BF16),
        in_specs=[vmem] * 6 + [hbm] * 5,
        out_specs=vmem,
        scratch_shapes=[
            pltpu.VMEM((width, units), BF16),
            pltpu.VMEM((width, units), BF16),
            pltpu.VMEM((units, width), BF16),
            pltpu.VMEM((width, 2, channels), BF16),
            pltpu.VMEM((narrow, width, 2 * channels), BF16),
            pltpu.VMEM((narrow * channels, width), BF16),
            pltpu.VMEM((frame_count, 128), F32),
            pltpu.VMEM((slot_count, dc), BF16),
            pltpu.VMEM((slot_count, width), BF16),
            pltpu.VMEM((rows, units), BF16),
            pltpu.VMEM((slot_count, width), BF16),
            pltpu.VMEM((narrow, slot_count, dc), BF16),
            pltpu.VMEM((slot_count, dc), BF16),
            pltpu.VMEM((slot_count, dc), BF16),
            pltpu.VMEM((frame_count, dc), F32),
            pltpu.VMEM((frame_count, dc), F32),
            pltpu.VMEM((frame_count, width), BF16),
            pltpu.VMEM((share, width), F32),
            pltpu.VMEM((share + 2 * HALO, narrow * channels), BF16),
            pltpu.VMEM((share + 2 * HALO, narrow * channels), F32),
            pltpu.VMEM((share, narrow * channels), BF16),
            pltpu.VMEM((narrow, -(-depth_kernel.shape[0] // 8) * 8, channels), F32),
            dma((5,)),
            dma((wide,)),
            dma((wide,)),
            dma((groups, narrow)),
            dma((groups, narrow)),
            dma((groups, narrow)),
            dma((groups, narrow)),
            dma((wide,)),
            dma((wide,)),
            dma((narrow,)),
            dma((narrow,)),
            dma((2,)),
            dma((2,)),
            dma((narrow,)),
            dma((narrow,)),
            dma((narrow,)),
            dma((narrow,)),
            dma((narrow,)),
            dma((narrow,)),
        ],
        compiler_params=pltpu.CompilerParams(
            collective_id=0, has_side_effects=True, vmem_limit_bytes=56 * 1024 * 1024
        ),
        cost_estimate=pl.CostEstimate(
            flops=flops, bytes_accessed=2 * 3 * width * units, transcendentals=0
        ),
        name="conformer_block",
    )(
        frames,
        expert_ids.T,
        gate_values.T,
        norm_gain.reshape(1, width),
        norm_bias.reshape(1, width),
        depth_kernel,
        w_gate,
        w_up,
        w_down,
        point_in,
        point_out,
    )


def solution(mesh):
    return jax.shard_map(
        shards,
        mesh=mesh,
        in_specs=(
            P("wide", None),
            P("wide", None),
            P("wide", None),
            P("wide", None, "narrow"),
            P("wide", None, "narrow"),
            P("wide", "narrow", None),
            P(),
            P(),
            P(None, None, "narrow"),
            P(None, "narrow"),
            P("narrow", None),
        ),
        out_specs=P(("wide", "narrow"), None),
        check_vma=False,
    )
```

```python
import functools

import jax
import jax.numpy as jnp
from jax import lax
from jax.experimental import pallas as pl
from jax.experimental.pallas import tpu as pltpu
from jax.sharding import PartitionSpec as P

F32 = jnp.float32
BF16 = jnp.bfloat16
HALO = 16


def block_kernel(
    wide,
    narrow,
    groups,
    cap,
    frames_ref,
    ids_ref,
    gates_ref,
    gain_ref,
    bias_ref,
    depth_ref,
    w_gate_hbm,
    w_up_hbm,
    w_down_hbm,
    pin_hbm,
    pout_hbm,
    out_ref,
    w_gate,
    w_up,
    w_down,
    pin_raw,
    pin,
    pout,
    turned,
    meta,
    far_meta,
    far_frames,
    outgoing,
    arrived,
    hidden,
    partial,
    partial_in,
    sums,
    returned,
    mix0,
    mix1,
    mixed,
    residual,
    padded,
    padded32,
    activated,
    shares,
    shares_in,
    w_sem,
    zs,
    zr,
    fs,
    fr,
    xs,
    xr,
    ps,
    pr,
    rs,
    rr,
    ms,
    mr,
    hs,
    hr,
    os_,
    or_,
):
    me_w = lax.axis_index("wide")
    me_n = lax.axis_index("narrow")
    frame_count, width = frames_ref.shape
    dc = width // narrow
    size = wide // groups
    rows = size * cap
    plane = me_w // size
    inner = me_w % size
    units = w_gate.shape[1]
    channels = pout.shape[0]
    share = frame_count // narrow
    taps = depth_ref.shape[0]

    def cols(index):
        return pl.ds(pl.multiple_of(index * dc, 128), dc)

    def slots(index):
        return pl.ds(pl.multiple_of(index * cap, 16), cap)

    def group_rows(index):
        return pl.ds(pl.multiple_of(index * rows, 16), rows)

    def share_rows(index):
        return pl.ds(pl.multiple_of(index * share, 16), share)

    my_cols = cols(me_n)

    barrier = pltpu.get_barrier_semaphore()

    def greet(i, carry):
        pl.semaphore_signal(
            barrier,
            inc=1,
            device_id=((me_w + i) % wide, me_n),
            device_id_type=pl.DeviceIdType.MESH,
        )
        return carry

    lax.fori_loop(1, wide, greet, 0)
    for i in range(1, narrow):
        pl.semaphore_signal(
            barrier,
            inc=1,
            device_id=(me_w, (me_n + i) % narrow),
            device_id_type=pl.DeviceIdType.MESH,
        )

    loads = [
        pltpu.make_async_copy(w_gate_hbm.at[0], w_gate, w_sem.at[0]),
        pltpu.make_async_copy(w_up_hbm.at[0], w_up, w_sem.at[1]),
        pltpu.make_async_copy(w_down_hbm.at[0], w_down, w_sem.at[2]),
        pltpu.make_async_copy(pin_hbm, pin_raw, w_sem.at[3]),
        pltpu.make_async_copy(pout_hbm, pout, w_sem.at[4]),
    ]
    for load in loads:
        load.start()

    def remote(src, dst, send, recv, device):
        return pltpu.make_async_remote_copy(
            src_ref=src,
            dst_ref=dst,
            send_sem=send,
            recv_sem=recv,
            device_id=device,
            device_id_type=pl.DeviceIdType.MESH,
        )

    partner = (plane + 2) % groups * size + inner
    pl.semaphore_wait(barrier, wide - 1 + narrow - 1)
    far_copy = remote(
        frames_ref.at[:, my_cols], far_frames, zs.at[0], zr.at[0], (partner, me_n)
    )
    far_copy.start()
    meta_copy = remote(meta, far_meta, zs.at[1], zr.at[1], (partner, me_n))

    id0 = ids_ref[0:1, :]
    id1 = ids_ref[1:2, :]
    lane = lax.broadcasted_iota(jnp.int32, (128, frame_count), 0)
    named0 = lane == id0
    named1 = lane == id1
    named = jnp.where(named0 | named1, 1.0, 0.0).astype(BF16)
    earlier = jnp.where(
        lax.broadcasted_iota(jnp.int32, (frame_count, frame_count), 0)
        < lax.broadcasted_iota(jnp.int32, (frame_count, frame_count), 1),
        1.0,
        0.0,
    ).astype(BF16)
    position = jnp.dot(named, earlier, preferred_element_type=F32)
    row0 = id0.astype(F32) * cap + jnp.sum(
        jnp.where(named0, position, 0.0), axis=0, keepdims=True
    )
    row1 = id1.astype(F32) * cap + jnp.sum(
        jnp.where(named1, position, 0.0), axis=0, keepdims=True
    )
    stacked = jnp.where(
        lane == 0,
        row0,
        jnp.where(
            lane == 1, row1, jnp.where(lane == 2, gates_ref[0:1, :], gates_ref[1:2, :])
        ),
    )
    meta[...] = stacked[0:8, :]
    meta_copy.start()
    turned[...] = jnp.transpose(stacked)
    row0 = row0.astype(jnp.int32)
    row1 = row1.astype(jnp.int32)

    def crossing(g):
        return ((g + 1) // 2) % 2

    def plane_of(g):
        return ((plane // 2 + crossing(g)) % 2) * 2 + (plane % 2 + g // 2) % 2

    def near_plane(g):
        return plane // 2 * 2 + (plane % 2 + g // 2) % 2

    def send_copy(g, i):
        p = plane_of(g) * size + i
        home = me_w + crossing(g) * (partner - me_w)
        return remote(
            outgoing.at[slots(p), :],
            arrived.at[slots(home), my_cols],
            fs.at[p],
            fr.at[home],
            (near_plane(g) * size + i, me_n),
        )

    def recv_copy(g, i):
        s = plane_of(g) * size + i
        return remote(
            outgoing.at[slots(s), :],
            arrived.at[slots(s), my_cols],
            fs.at[s],
            fr.at[s],
            (near_plane(g) * size + i, me_n),
        )

    def dispatch(g, first, second, source):
        q = plane_of(g)
        place = lax.broadcasted_iota(jnp.int32, (rows, frame_count), 0) + near_plane(g) * rows
        choose = jnp.where((place == first) | (place == second), 1.0, 0.0).astype(BF16)
        outgoing[group_rows(q), :] = jnp.dot(
            choose, source, preferred_element_type=F32
        ).astype(BF16)
        local = g // 2 == 0
        if local:
            own = slots(q * size + inner)
            arrived[own, my_cols] = outgoing[own, :]

        def send(i, carry):
            send_copy(g, (inner + i) % size).start()
            return carry

        lax.fori_loop(1 if local else 0, size, send, 0)

    mine = frames_ref[:, my_cols]
    dispatch(3, row0, row1, mine)
    dispatch(0, row0, row1, mine)

    def forward_copy(g, q, m):
        part = arrived.at[group_rows(q), my_cols]
        return remote(part, part, xs.at[g, m], xr.at[g, me_n], (me_w, m))

    def forward_in(g, q, m):
        part = arrived.at[group_rows(q), cols(m)]
        return remote(part, part, xs.at[g, m], xr.at[g, m], (me_w, m))

    def partial_copy(g, q, m):
        return remote(
            partial.at[group_rows(q), cols(m)],
            partial_in.at[me_n, group_rows(q), :],
            ps.at[g, m],
            pr.at[g, me_n],
            (me_w, m),
        )

    def partial_wait(g, q, m):
        return remote(
            partial.at[group_rows(q), cols(m)],
            partial_in.at[m, group_rows(q), :],
            ps.at[g, m],
            pr.at[g, m],
            (me_w, m),
        )

    def return_copy(s):
        return remote(
            sums.at[slots(s), :],
            returned.at[slots(me_w), :],
            rs.at[s],
            rr.at[me_w],
            (s, me_n),
        )

    def return_wait(p):
        return remote(
            sums.at[slots(p), :],
            returned.at[slots(p), :],
            rs.at[p],
            rr.at[p],
            (p, me_n),
        )

    siblings = [(me_n + i) % narrow for i in range(1, narrow)]
    tile = min(512, units)

    def step(g, carry):
        q = plane_of(g)

        @pl.when(g == 1)
        def _():
            for load in loads[3:]:
                load.wait()

            def sort(i, c):
                r = pl.ds(pl.multiple_of(i * 64, 64), 64)
                pin[r, :channels] = pin_raw[r, 0, :]
                pin[r, channels:] = pin_raw[r, 1, :]
                return c

            lax.fori_loop(0, width // 64, sort, 0)
            far_copy.wait_recv()
            meta_copy.wait_recv()
            far0 = far_meta[0:1, :].astype(jnp.int32)
            far1 = far_meta[1:2, :].astype(jnp.int32)
            far = far_frames[...]
            dispatch(2, far0, far1, far)
            dispatch(1, far0, far1, far)

        def take(i, c):
            other = (inner + size - i) % size

            @pl.when(near_plane(g) * size + other != me_w)
            def _():
                recv_copy(g, other).wait_recv()

            return c

        lax.fori_loop(0, size, take, 0)
        for m in siblings:
            forward_copy(g, q, m).start()

        @pl.when(g == 0)
        def _():
            for load in loads[:3]:
                load.wait()

        for m in siblings:
            forward_in(g, q, m).wait_recv()

        x = arrived[group_rows(q), :]
        for f in range(0, units, tile):
            gate = jnp.dot(x, w_gate[:, f : f + tile], preferred_element_type=F32)
            up = jnp.dot(x, w_up[:, f : f + tile], preferred_element_type=F32)
            hidden[:, f : f + tile] = (gate * jax.nn.sigmoid(gate) * up).astype(BF16)
        for m in siblings:
            partial[group_rows(q), cols(m)] = jnp.dot(
                hidden[...], w_down[:, cols(m)], preferred_element_type=F32
            ).astype(BF16)
            partial_copy(g, q, m).start()
        total = jnp.dot(hidden[...], w_down[:, my_cols], preferred_element_type=F32)
        for m in siblings:
            partial_wait(g, q, m).wait_recv()
            total = total + partial_in[m, group_rows(q), :].astype(F32)
        sums[group_rows(q), :] = total.astype(BF16)

        def give(i, c):
            s = q * size + (inner + size - i) % size

            @pl.when(s != me_w)
            def _():
                return_copy(s).start()

            return c

        lax.fori_loop(0, size, give, 0)
        return carry

    lax.fori_loop(0, groups, step, 0)
    returned[slots(me_w), :] = sums[slots(me_w), :]

    mix0[...] = jnp.zeros_like(mix0)
    mix1[...] = jnp.zeros_like(mix1)

    def combine(g, carry):
        q = plane_of(g)

        def take(i, c):
            p = q * size + (inner + i) % size

            @pl.when(p != me_w)
            def _():
                return_wait(p).wait_recv()

            return c

        lax.fori_loop(0, size, take, 0)
        place = lax.broadcasted_iota(jnp.int32, (frame_count, rows), 1) + q * rows
        block = returned[group_rows(q), :]
        mix0[...] += jnp.dot(
            jnp.where(place == turned[:, 0:1].astype(jnp.int32), 1.0, 0.0).astype(BF16), block, preferred_element_type=F32
        )
        mix1[...] += jnp.dot(
            jnp.where(place == turned[:, 1:2].astype(jnp.int32), 1.0, 0.0).astype(BF16), block, preferred_element_type=F32
        )
        return carry

    lax.fori_loop(0, groups, combine, 0)
    mixed[:, my_cols] = (
        turned[:, 2:3] * mix0[...] + turned[:, 3:4] * mix1[...]
    ).astype(BF16)

    def mix_copy(m):
        part = mixed.at[:, my_cols]
        return remote(part, part, ms.at[m], mr.at[me_n], (me_w, m))

    def mix_wait(m):
        part = mixed.at[:, cols(m)]
        return remote(part, part, ms.at[m], mr.at[m], (me_w, m))

    for m in siblings:
        mix_copy(m).start()
    for m in siblings:
        mix_wait(m).wait_recv()

    res = frames_ref[...].astype(F32) + mixed[...].astype(F32)
    residual[...] = res
    centered = res - jnp.mean(res, axis=1, keepdims=True)
    variance = jnp.mean(centered * centered, axis=1, keepdims=True)
    normed = (centered * lax.rsqrt(variance + 1e-05) * gain_ref[...] + bias_ref[...]).astype(BF16)
    value_half = jnp.dot(normed, pin[:, :channels], preferred_element_type=F32)
    gate_half = jnp.dot(normed, pin[:, channels:], preferred_element_type=F32)
    glu = (value_half * jax.nn.sigmoid(gate_half)).astype(BF16)
    padded[HALO : HALO + frame_count, :] = glu
    padded32[HALO : HALO + frame_count, :] = glu.astype(F32)

    end = HALO + frame_count
    to_left = remote(
        padded.at[HALO : 2 * HALO, :],
        padded.at[end : end + HALO, :],
        hs.at[0],
        hr.at[0],
        ((me_w + wide - 1) % wide, me_n),
    )
    to_right = remote(
        padded.at[frame_count:end, :],
        padded.at[0:HALO, :],
        hs.at[1],
        hr.at[1],
        ((me_w + 1) % wide, me_n),
    )
    has_left = me_w > 0
    has_right = me_w < wide - 1

    @pl.when(has_left)
    def _():
        to_left.start()

    @pl.when(has_right)
    def _():
        to_right.start()

    half = (taps - 1) // 2
    step_rows = 64

    def depthwise(starts):
        def strip(c, carry):
            lanes = pl.ds(pl.multiple_of(c * 128, 128), 128)
            kernel_taps = depth_ref[:, lanes].astype(F32)
            for start in starts:
                total = jnp.zeros((step_rows, 128), F32)
                for j in range(taps):
                    low = start + HALO - half + j
                    total = total + padded32[low : low + step_rows, lanes] * kernel_taps[j : j + 1, :]
                activated[start : start + step_rows, lanes] = (
                    total * jax.nn.sigmoid(total)
                ).astype(BF16)
            return carry

        lax.fori_loop(0, channels // 128, strip, 0)

    depthwise(range(step_rows, frame_count - step_rows, step_rows))

    @pl.when(has_right)
    def _():
        to_left.wait_recv()
        padded32[end : end + HALO, :] = padded[end : end + HALO, :].astype(F32)

    @pl.when(jnp.logical_not(has_right))
    def _():
        padded32[end : end + HALO, :] = jnp.zeros((HALO, channels), F32)

    @pl.when(has_left)
    def _():
        to_right.wait_recv()
        padded32[0:HALO, :] = padded[0:HALO, :].astype(F32)

    @pl.when(jnp.logical_not(has_left))
    def _():
        padded32[0:HALO, :] = jnp.zeros((HALO, channels), F32)

    depthwise((0, frame_count - step_rows))

    def share_copy(m):
        return remote(
            shares.at[share_rows(m), :], shares_in.at[me_n], os_.at[m], or_.at[me_n], (me_w, m)
        )

    def share_wait(m):
        return remote(
            shares.at[share_rows(m), :], shares_in.at[m], os_.at[m], or_.at[m], (me_w, m)
        )

    for m in siblings:
        shares[share_rows(m), :] = jnp.dot(
            activated[share_rows(m), :], pout[...], preferred_element_type=F32
        ).astype(BF16)
        share_copy(m).start()
    total = residual[share_rows(me_n), :] + jnp.dot(
        activated[share_rows(me_n), :], pout[...], preferred_element_type=F32
    )
    for m in siblings:
        share_wait(m).wait_recv()
        total = total + shares_in[m].astype(F32)
    out_ref[...] = total.astype(BF16)

    def finish(i, carry):
        return_copy((me_w + i) % wide).wait_send()
        return carry

    lax.fori_loop(1, wide, finish, 0)
    for m in siblings:
        mix_copy(m).wait_send()
        share_copy(m).wait_send()

    far_copy.wait_send()
    meta_copy.wait_send()

    def finish_group(g, carry):
        q = plane_of(g)

        def sent(i, c):
            @pl.when(near_plane(g) * size + i != me_w)
            def _():
                send_copy(g, i).wait_send()

            return c

        lax.fori_loop(0, size, sent, 0)
        for m in siblings:
            forward_copy(g, q, m).wait_send()
            partial_copy(g, q, m).wait_send()
        return carry

    lax.fori_loop(0, groups, finish_group, 0)

    @pl.when(has_left)
    def _():
        to_left.wait_send()

    @pl.when(has_right)
    def _():
        to_right.wait_send()


def shards(
    frames,
    expert_ids,
    gate_values,
    w_gate,
    w_up,
    w_down,
    norm_gain,
    norm_bias,
    point_in,
    depth_kernel,
    point_out,
):
    frame_count, width = frames.shape
    top_count = expert_ids.shape[1]
    wide = lax.axis_size("wide")
    narrow = lax.axis_size("narrow")
    expert_count = w_gate.shape[0] * wide
    cap = 2 * top_count * frame_count // expert_count
    units = w_gate.shape[2]
    channels = point_in.shape[2]
    groups = 4
    slot_count = wide * cap
    rows = slot_count // groups
    dc = width // narrow
    share = frame_count // narrow
    vmem = pl.BlockSpec(memory_space=pltpu.VMEM)
    hbm = pl.BlockSpec(memory_space=pl.ANY)
    dma = pltpu.SemaphoreType.DMA
    flops = 2 * width * (3 * slot_count * units + 3 * frame_count * channels)
    return pl.pallas_call(
        functools.partial(block_kernel, wide, narrow, groups, cap),
        out_shape=jax.ShapeDtypeStruct((share, width), BF16),
        in_specs=[vmem] * 6 + [hbm] * 5,
        out_specs=vmem,
        scratch_shapes=[
            pltpu.VMEM((width, units), BF16),
            pltpu.VMEM((width, units), BF16),
            pltpu.VMEM((units, width), BF16),
            pltpu.VMEM((width, 2, channels), BF16),
            pltpu.VMEM((width, 2 * channels), BF16),
            pltpu.VMEM((channels, width), BF16),
            pltpu.VMEM((frame_count, 128), F32),
            pltpu.VMEM((8, frame_count), F32),
            pltpu.VMEM((8, frame_count), F32),
            pltpu.VMEM((frame_count, dc), BF16),
            pltpu.VMEM((slot_count, dc), BF16),
            pltpu.VMEM((slot_count, width), BF16),
            pltpu.VMEM((rows, units), BF16),
            pltpu.VMEM((slot_count, width), BF16),
            pltpu.VMEM((narrow, slot_count, dc), BF16),
            pltpu.VMEM((slot_count, dc), BF16),
            pltpu.VMEM((slot_count, dc), BF16),
            pltpu.VMEM((frame_count, dc), F32),
            pltpu.VMEM((frame_count, dc), F32),
            pltpu.VMEM((frame_count, width), BF16),
            pltpu.VMEM((frame_count, width), F32),
            pltpu.VMEM((frame_count + 2 * HALO, channels), BF16),
            pltpu.VMEM((frame_count + 2 * HALO, channels), F32),
            pltpu.VMEM((frame_count, channels), BF16),
            pltpu.VMEM((frame_count, width), BF16),
            pltpu.VMEM((narrow, share, width), BF16),
            dma((5,)),
            dma((2,)),
            dma((2,)),
            dma((wide,)),
            dma((wide,)),
            dma((groups, narrow)),
            dma((groups, narrow)),
            dma((groups, narrow)),
            dma((groups, narrow)),
            dma((wide,)),
            dma((wide,)),
            dma((narrow,)),
            dma((narrow,)),
            dma((2,)),
            dma((2,)),
            dma((narrow,)),
            dma((narrow,)),
        ],
        compiler_params=pltpu.CompilerParams(
            collective_id=0, has_side_effects=True, vmem_limit_bytes=56 * 1024 * 1024
        ),
        cost_estimate=pl.CostEstimate(
            flops=flops, bytes_accessed=2 * 3 * width * units, transcendentals=0
        ),
        name="conformer_block",
    )(
        frames,
        expert_ids.T,
        gate_values.T,
        norm_gain.reshape(1, width),
        norm_bias.reshape(1, width),
        depth_kernel,
        w_gate,
        w_up,
        w_down,
        point_in,
        point_out,
    )


def solution(mesh):
    return jax.shard_map(
        shards,
        mesh=mesh,
        in_specs=(
            P("wide", None),
            P("wide", None),
            P("wide", None),
            P("wide", None, "narrow"),
            P("wide", None, "narrow"),
            P("wide", "narrow", None),
            P(),
            P(),
            P(None, None, "narrow"),
            P(None, "narrow"),
            P("narrow", None),
        ),
        out_specs=P(("wide", "narrow"), None),
        check_vma=False,
    )
```

```python
import functools

import jax
import jax.numpy as jnp
from jax import lax
from jax.experimental import pallas as pl
from jax.experimental.pallas import tpu as pltpu
from jax.sharding import PartitionSpec as P

F32 = jnp.float32
BF16 = jnp.bfloat16
HALO = 16


def block_kernel(
    wide,
    narrow,
    groups,
    cap,
    frames_ref,
    ids_ref,
    gates_ref,
    gain_ref,
    bias_ref,
    depth_ref,
    w_gate_hbm,
    w_up_hbm,
    w_down_hbm,
    pin_hbm,
    pout_hbm,
    out_ref,
    w_gate,
    w_up,
    w_down,
    pin_raw,
    pin,
    pout,
    turned,
    own,
    outgoing,
    arrived,
    hidden,
    partial,
    partial_in,
    sums,
    returned,
    mix0,
    mix1,
    mixed,
    residual,
    padded,
    padded32,
    activated,
    shares,
    shares_in,
    w_sem,
    fs,
    fr,
    xs,
    xr,
    ps,
    pr,
    rs,
    rr,
    ms,
    mr,
    hs,
    hr,
    os_,
    or_,
):
    me_w = lax.axis_index("wide")
    me_n = lax.axis_index("narrow")
    frame_count, width = frames_ref.shape
    dc = width // narrow
    size = wide // groups
    rows = size * cap
    plane = me_w // size
    inner = me_w % size
    units = w_gate.shape[1]
    channels = pout.shape[0]
    share = frame_count // narrow
    taps = depth_ref.shape[0]

    def cols(index):
        return pl.ds(pl.multiple_of(index * dc, 128), dc)

    def slots(index):
        return pl.ds(pl.multiple_of(index * cap, 16), cap)

    def group_rows(index):
        return pl.ds(pl.multiple_of(index * rows, 16), rows)

    def share_rows(index):
        return pl.ds(pl.multiple_of(index * share, 16), share)

    my_cols = cols(me_n)

    barrier = pltpu.get_barrier_semaphore()

    def greet(i, carry):
        pl.semaphore_signal(
            barrier,
            inc=1,
            device_id=((me_w + i) % wide, me_n),
            device_id_type=pl.DeviceIdType.MESH,
        )
        return carry

    lax.fori_loop(1, wide, greet, 0)
    for i in range(1, narrow):
        pl.semaphore_signal(
            barrier,
            inc=1,
            device_id=(me_w, (me_n + i) % narrow),
            device_id_type=pl.DeviceIdType.MESH,
        )

    loads = [
        pltpu.make_async_copy(w_gate_hbm.at[0], w_gate, w_sem.at[0]),
        pltpu.make_async_copy(w_up_hbm.at[0], w_up, w_sem.at[1]),
        pltpu.make_async_copy(w_down_hbm.at[0], w_down, w_sem.at[2]),
        pltpu.make_async_copy(pin_hbm, pin_raw, w_sem.at[3]),
        pltpu.make_async_copy(pout_hbm, pout, w_sem.at[4]),
    ]
    for load in loads:
        load.start()

    def remote(src, dst, send, recv, device):
        return pltpu.make_async_remote_copy(
            src_ref=src,
            dst_ref=dst,
            send_sem=send,
            recv_sem=recv,
            device_id=device,
            device_id_type=pl.DeviceIdType.MESH,
        )

    id0 = ids_ref[0:1, :]
    id1 = ids_ref[1:2, :]
    lane = lax.broadcasted_iota(jnp.int32, (128, frame_count), 0)
    named0 = lane == id0
    named1 = lane == id1
    named = jnp.where(named0 | named1, 1.0, 0.0).astype(BF16)
    earlier = jnp.where(
        lax.broadcasted_iota(jnp.int32, (frame_count, frame_count), 0)
        < lax.broadcasted_iota(jnp.int32, (frame_count, frame_count), 1),
        1.0,
        0.0,
    ).astype(BF16)
    position = jnp.dot(named, earlier, preferred_element_type=F32)
    row0 = id0.astype(F32) * cap + jnp.sum(
        jnp.where(named0, position, 0.0), axis=0, keepdims=True
    )
    row1 = id1.astype(F32) * cap + jnp.sum(
        jnp.where(named1, position, 0.0), axis=0, keepdims=True
    )
    stacked = jnp.where(
        lane == 0,
        row0,
        jnp.where(
            lane == 1, row1, jnp.where(lane == 2, gates_ref[0:1, :], gates_ref[1:2, :])
        ),
    )
    turned[...] = jnp.transpose(stacked)
    row0 = row0.astype(jnp.int32)
    row1 = row1.astype(jnp.int32)

    def plane_of(g):
        return ((plane // 2 + g % 2) % 2) * 2 + (plane % 2 + g // 2) % 2

    def send_copy(p):
        return remote(
            outgoing.at[slots(p), :],
            arrived.at[slots(me_w), my_cols],
            fs.at[p],
            fr.at[me_w],
            (p, me_n),
        )

    def recv_copy(s):
        return remote(
            outgoing.at[slots(s), :],
            arrived.at[slots(s), my_cols],
            fs.at[s],
            fr.at[s],
            (s, me_n),
        )

    mine = frames_ref[:, my_cols]
    for turn, g in enumerate((1, 0, 3, 2)):
        q = plane_of(g)
        place = lax.broadcasted_iota(jnp.int32, (rows, frame_count), 0) + q * rows
        choose = jnp.where((place == row0) | (place == row1), 1.0, 0.0).astype(BF16)
        outgoing[group_rows(q), :] = jnp.dot(
            choose, mine, preferred_element_type=F32
        ).astype(BF16)
        if turn == 0:
            pl.semaphore_wait(barrier, wide - 1 + narrow - 1)
        if g == 0:
            arrived[slots(me_w), my_cols] = outgoing[slots(me_w), :]

        def send(i, carry, q=q):
            send_copy(q * size + (inner + i) % size).start()
            return carry

        lax.fori_loop(1 if g == 0 else 0, size, send, 0)

    def forward_copy(g, q, m):
        part = arrived.at[group_rows(q), my_cols]
        return remote(part, part, xs.at[g, m], xr.at[g, me_n], (me_w, m))

    def forward_in(g, q, m):
        part = arrived.at[group_rows(q), cols(m)]
        return remote(part, part, xs.at[g, m], xr.at[g, m], (me_w, m))

    def partial_copy(g, q, m):
        return remote(
            partial.at[group_rows(q), cols(m)],
            partial_in.at[me_n, group_rows(q), :],
            ps.at[g, m],
            pr.at[g, me_n],
            (me_w, m),
        )

    def partial_wait(g, q, m):
        return remote(
            partial.at[group_rows(q), cols(m)],
            partial_in.at[m, group_rows(q), :],
            ps.at[g, m],
            pr.at[g, m],
            (me_w, m),
        )

    def return_copy(s):
        return remote(
            sums.at[slots(s), :],
            returned.at[slots(me_w), :],
            rs.at[s],
            rr.at[me_w],
            (s, me_n),
        )

    def return_wait(p):
        return remote(
            sums.at[slots(p), :],
            returned.at[slots(p), :],
            rs.at[p],
            rr.at[p],
            (p, me_n),
        )

    siblings = [(me_n + i) % narrow for i in range(1, narrow)]
    tile = min(512, units)

    def take_in(g):
        q = plane_of(g)

        def take(i, c):
            s = q * size + (inner + size - i) % size

            @pl.when(s != me_w)
            def _():
                recv_copy(s).wait_recv()

            return c

        lax.fori_loop(0, size, take, 0)
        for m in siblings:
            forward_copy(g, q, m).start()

    def give_back(g):
        q = plane_of(g)
        total = own[...]
        for m in siblings:
            partial_wait(g, q, m).wait_recv()
            total = total + partial_in[m, group_rows(q), :].astype(F32)
        sums[group_rows(q), :] = total.astype(BF16)

        def give(i, c):
            s = q * size + (inner + size - i) % size

            @pl.when(s != me_w)
            def _():
                return_copy(s).start()

            return c

        lax.fori_loop(0, size, give, 0)

    take_in(0)
    for load in loads[:3]:
        load.wait()

    def step(g, carry):
        q = plane_of(g)
        for m in siblings:
            forward_in(g, q, m).wait_recv()
        x = arrived[group_rows(q), :]
        for f in range(0, units, tile):
            gate = jnp.dot(x, w_gate[:, f : f + tile], preferred_element_type=F32)
            up = jnp.dot(x, w_up[:, f : f + tile], preferred_element_type=F32)
            hidden[:, f : f + tile] = (gate * jax.nn.sigmoid(gate) * up).astype(BF16)

        @pl.when(g > 0)
        def _():
            give_back(g - 1)

        @pl.when(g < groups - 1)
        def _():
            take_in(g + 1)

        for m in siblings:
            partial[group_rows(q), cols(m)] = jnp.dot(
                hidden[...], w_down[:, cols(m)], preferred_element_type=F32
            ).astype(BF16)
            partial_copy(g, q, m).start()
        own[...] = jnp.dot(hidden[...], w_down[:, my_cols], preferred_element_type=F32)
        return carry

    lax.fori_loop(0, groups, step, 0)
    give_back(groups - 1)

    for load in loads[3:]:
        load.wait()

    def sort(i, c):
        r = pl.ds(pl.multiple_of(i * 64, 64), 64)
        pin[r, :channels] = pin_raw[r, 0, :]
        pin[r, channels:] = pin_raw[r, 1, :]
        return c

    lax.fori_loop(0, width // 64, sort, 0)
    returned[slots(me_w), :] = sums[slots(me_w), :]

    mix0[...] = jnp.zeros_like(mix0)
    mix1[...] = jnp.zeros_like(mix1)

    def combine(g, carry):
        q = plane_of(g)

        def take(i, c):
            p = q * size + (inner + i) % size

            @pl.when(p != me_w)
            def _():
                return_wait(p).wait_recv()

            return c

        lax.fori_loop(0, size, take, 0)
        place = lax.broadcasted_iota(jnp.int32, (frame_count, rows), 1) + q * rows
        block = returned[group_rows(q), :]
        mix0[...] += jnp.dot(
            jnp.where(place == turned[:, 0:1].astype(jnp.int32), 1.0, 0.0).astype(BF16), block, preferred_element_type=F32
        )
        mix1[...] += jnp.dot(
            jnp.where(place == turned[:, 1:2].astype(jnp.int32), 1.0, 0.0).astype(BF16), block, preferred_element_type=F32
        )
        return carry

    lax.fori_loop(0, groups, combine, 0)
    mixed[:, my_cols] = (
        turned[:, 2:3] * mix0[...] + turned[:, 3:4] * mix1[...]
    ).astype(BF16)

    def mix_copy(m):
        part = mixed.at[:, my_cols]
        return remote(part, part, ms.at[m], mr.at[me_n], (me_w, m))

    def mix_wait(m):
        part = mixed.at[:, cols(m)]
        return remote(part, part, ms.at[m], mr.at[m], (me_w, m))

    for m in siblings:
        mix_copy(m).start()
    for m in siblings:
        mix_wait(m).wait_recv()

    res = frames_ref[...].astype(F32) + mixed[...].astype(F32)
    residual[...] = res
    centered = res - jnp.mean(res, axis=1, keepdims=True)
    variance = jnp.mean(centered * centered, axis=1, keepdims=True)
    normed = (centered * lax.rsqrt(variance + 1e-05) * gain_ref[...] + bias_ref[...]).astype(BF16)
    value_half = jnp.dot(normed, pin[:, :channels], preferred_element_type=F32)
    gate_half = jnp.dot(normed, pin[:, channels:], preferred_element_type=F32)
    glu = (value_half * jax.nn.sigmoid(gate_half)).astype(BF16)
    padded[HALO : HALO + frame_count, :] = glu
    padded32[HALO : HALO + frame_count, :] = glu.astype(F32)

    end = HALO + frame_count
    to_left = remote(
        padded.at[HALO : 2 * HALO, :],
        padded.at[end : end + HALO, :],
        hs.at[0],
        hr.at[0],
        ((me_w + wide - 1) % wide, me_n),
    )
    to_right = remote(
        padded.at[frame_count:end, :],
        padded.at[0:HALO, :],
        hs.at[1],
        hr.at[1],
        ((me_w + 1) % wide, me_n),
    )
    has_left = me_w > 0
    has_right = me_w < wide - 1

    @pl.when(has_left)
    def _():
        to_left.start()

    @pl.when(has_right)
    def _():
        to_right.start()

    half = (taps - 1) // 2
    step_rows = 64

    def depthwise(starts):
        def strip(c, carry):
            lanes = pl.ds(pl.multiple_of(c * 128, 128), 128)
            kernel_taps = depth_ref[:, lanes].astype(F32)
            for start in starts:
                total = jnp.zeros((step_rows, 128), F32)
                for j in range(taps):
                    low = start + HALO - half + j
                    total = total + padded32[low : low + step_rows, lanes] * kernel_taps[j : j + 1, :]
                activated[start : start + step_rows, lanes] = (
                    total * jax.nn.sigmoid(total)
                ).astype(BF16)
            return carry

        lax.fori_loop(0, channels // 128, strip, 0)

    depthwise(range(step_rows, frame_count - step_rows, step_rows))

    @pl.when(has_right)
    def _():
        to_left.wait_recv()
        padded32[end : end + HALO, :] = padded[end : end + HALO, :].astype(F32)

    @pl.when(jnp.logical_not(has_right))
    def _():
        padded32[end : end + HALO, :] = jnp.zeros((HALO, channels), F32)

    @pl.when(has_left)
    def _():
        to_right.wait_recv()
        padded32[0:HALO, :] = padded[0:HALO, :].astype(F32)

    @pl.when(jnp.logical_not(has_left))
    def _():
        padded32[0:HALO, :] = jnp.zeros((HALO, channels), F32)

    depthwise((0, frame_count - step_rows))

    def share_copy(m):
        return remote(
            shares.at[share_rows(m), :], shares_in.at[me_n], os_.at[m], or_.at[me_n], (me_w, m)
        )

    def share_wait(m):
        return remote(
            shares.at[share_rows(m), :], shares_in.at[m], os_.at[m], or_.at[m], (me_w, m)
        )

    for m in siblings:
        shares[share_rows(m), :] = jnp.dot(
            activated[share_rows(m), :], pout[...], preferred_element_type=F32
        ).astype(BF16)
        share_copy(m).start()
    total = residual[share_rows(me_n), :] + jnp.dot(
        activated[share_rows(me_n), :], pout[...], preferred_element_type=F32
    )
    for m in siblings:
        share_wait(m).wait_recv()
        total = total + shares_in[m].astype(F32)
    out_ref[...] = total.astype(BF16)

    def finish(i, carry):
        p = (me_w + i) % wide
        send_copy(p).wait_send()
        return_copy(p).wait_send()
        return carry

    lax.fori_loop(1, wide, finish, 0)
    for m in siblings:
        mix_copy(m).wait_send()
        share_copy(m).wait_send()

    def finish_group(g, carry):
        q = plane_of(g)
        for m in siblings:
            forward_copy(g, q, m).wait_send()
            partial_copy(g, q, m).wait_send()
        return carry

    lax.fori_loop(0, groups, finish_group, 0)

    @pl.when(has_left)
    def _():
        to_left.wait_send()

    @pl.when(has_right)
    def _():
        to_right.wait_send()


def shards(
    frames,
    expert_ids,
    gate_values,
    w_gate,
    w_up,
    w_down,
    norm_gain,
    norm_bias,
    point_in,
    depth_kernel,
    point_out,
):
    frame_count, width = frames.shape
    top_count = expert_ids.shape[1]
    wide = lax.axis_size("wide")
    narrow = lax.axis_size("narrow")
    expert_count = w_gate.shape[0] * wide
    cap = 2 * top_count * frame_count // expert_count
    units = w_gate.shape[2]
    channels = point_in.shape[2]
    groups = 4
    slot_count = wide * cap
    rows = slot_count // groups
    dc = width // narrow
    share = frame_count // narrow
    vmem = pl.BlockSpec(memory_space=pltpu.VMEM)
    hbm = pl.BlockSpec(memory_space=pl.ANY)
    dma = pltpu.SemaphoreType.DMA
    flops = 2 * width * (3 * slot_count * units + 3 * frame_count * channels)
    return pl.pallas_call(
        functools.partial(block_kernel, wide, narrow, groups, cap),
        out_shape=jax.ShapeDtypeStruct((share, width), BF16),
        in_specs=[vmem] * 6 + [hbm] * 5,
        out_specs=vmem,
        scratch_shapes=[
            pltpu.VMEM((width, units), BF16),
            pltpu.VMEM((width, units), BF16),
            pltpu.VMEM((units, width), BF16),
            pltpu.VMEM((width, 2, channels), BF16),
            pltpu.VMEM((width, 2 * channels), BF16),
            pltpu.VMEM((channels, width), BF16),
            pltpu.VMEM((frame_count, 128), F32),
            pltpu.VMEM((rows, dc), F32),
            pltpu.VMEM((slot_count, dc), BF16),
            pltpu.VMEM((slot_count, width), BF16),
            pltpu.VMEM((rows, units), BF16),
            pltpu.VMEM((slot_count, width), BF16),
            pltpu.VMEM((narrow, slot_count, dc), BF16),
            pltpu.VMEM((slot_count, dc), BF16),
            pltpu.VMEM((slot_count, dc), BF16),
            pltpu.VMEM((frame_count, dc), F32),
            pltpu.VMEM((frame_count, dc), F32),
            pltpu.VMEM((frame_count, width), BF16),
            pltpu.VMEM((frame_count, width), F32),
            pltpu.VMEM((frame_count + 2 * HALO, channels), BF16),
            pltpu.VMEM((frame_count + 2 * HALO, channels), F32),
            pltpu.VMEM((frame_count, channels), BF16),
            pltpu.VMEM((frame_count, width), BF16),
            pltpu.VMEM((narrow, share, width), BF16),
            dma((5,)),
            dma((wide,)),
            dma((wide,)),
            dma((groups, narrow)),
            dma((groups, narrow)),
            dma((groups, narrow)),
            dma((groups, narrow)),
            dma((wide,)),
            dma((wide,)),
            dma((narrow,)),
            dma((narrow,)),
            dma((2,)),
            dma((2,)),
            dma((narrow,)),
            dma((narrow,)),
        ],
        compiler_params=pltpu.CompilerParams(
            collective_id=0, has_side_effects=True, vmem_limit_bytes=56 * 1024 * 1024
        ),
        cost_estimate=pl.CostEstimate(
            flops=flops, bytes_accessed=2 * 3 * width * units, transcendentals=0
        ),
        name="conformer_block",
    )(
        frames,
        expert_ids.T,
        gate_values.T,
        norm_gain.reshape(1, width),
        norm_bias.reshape(1, width),
        depth_kernel,
        w_gate,
        w_up,
        w_down,
        point_in,
        point_out,
    )


def solution(mesh):
    return jax.shard_map(
        shards,
        mesh=mesh,
        in_specs=(
            P("wide", None),
            P("wide", None),
            P("wide", None),
            P("wide", None, "narrow"),
            P("wide", None, "narrow"),
            P("wide", "narrow", None),
            P(),
            P(),
            P(None, None, "narrow"),
            P(None, "narrow"),
            P("narrow", None),
        ),
        out_specs=P(("wide", "narrow"), None),
        check_vma=False,
    )
```

```python
import functools

import jax
import jax.numpy as jnp
from jax import lax
from jax.experimental import pallas as pl
from jax.experimental.pallas import tpu as pltpu
from jax.sharding import PartitionSpec as P

F32 = jnp.float32
BF16 = jnp.bfloat16
HALO = 16


def block_kernel(
    wide,
    narrow,
    groups,
    cap,
    frames_ref,
    ids_ref,
    gates_ref,
    gain_ref,
    bias_ref,
    depth_ref,
    w_gate_hbm,
    w_up_hbm,
    w_down_hbm,
    pin_hbm,
    pout_hbm,
    out_ref,
    w_gate,
    w_up,
    w_down,
    pin_raw,
    pin,
    pout,
    turned,
    own,
    outgoing,
    arrived,
    hidden,
    partial,
    partial_in,
    sums,
    returned,
    mix0,
    mix1,
    mixed,
    residual,
    padded,
    padded32,
    activated,
    shares,
    shares_in,
    w_sem,
    fs,
    fr,
    xs,
    xr,
    ps,
    pr,
    rs,
    rr,
    ms,
    mr,
    hs,
    hr,
    os_,
    or_,
):
    me_w = lax.axis_index("wide")
    me_n = lax.axis_index("narrow")
    frame_count, width = frames_ref.shape
    dc = width // narrow
    size = wide // groups
    rows = size * cap
    plane = me_w // size
    inner = me_w % size
    units = w_gate.shape[1]
    channels = pout.shape[0]
    share = frame_count // narrow
    taps = depth_ref.shape[0]

    def cols(index):
        return pl.ds(pl.multiple_of(index * dc, 128), dc)

    def slots(index):
        return pl.ds(pl.multiple_of(index * cap, 16), cap)

    def group_rows(index):
        return pl.ds(pl.multiple_of(index * rows, 16), rows)

    def share_rows(index):
        return pl.ds(pl.multiple_of(index * share, 16), share)

    my_cols = cols(me_n)

    barrier = pltpu.get_barrier_semaphore()

    def greet(i, carry):
        pl.semaphore_signal(
            barrier,
            inc=1,
            device_id=((me_w + i) % wide, me_n),
            device_id_type=pl.DeviceIdType.MESH,
        )
        return carry

    lax.fori_loop(1, wide, greet, 0)
    for i in range(1, narrow):
        pl.semaphore_signal(
            barrier,
            inc=1,
            device_id=(me_w, (me_n + i) % narrow),
            device_id_type=pl.DeviceIdType.MESH,
        )

    loads = [
        pltpu.make_async_copy(w_gate_hbm.at[0], w_gate, w_sem.at[0]),
        pltpu.make_async_copy(w_up_hbm.at[0], w_up, w_sem.at[1]),
        pltpu.make_async_copy(w_down_hbm.at[0], w_down, w_sem.at[2]),
        pltpu.make_async_copy(pin_hbm, pin_raw, w_sem.at[3]),
        pltpu.make_async_copy(pout_hbm, pout, w_sem.at[4]),
    ]
    for load in loads:
        load.start()

    def remote(src, dst, send, recv, device):
        return pltpu.make_async_remote_copy(
            src_ref=src,
            dst_ref=dst,
            send_sem=send,
            recv_sem=recv,
            device_id=device,
            device_id_type=pl.DeviceIdType.MESH,
        )

    id0 = ids_ref[0:1, :]
    id1 = ids_ref[1:2, :]
    lane = lax.broadcasted_iota(jnp.int32, (128, frame_count), 0)
    named0 = lane == id0
    named1 = lane == id1
    named = jnp.where(named0 | named1, 1.0, 0.0).astype(BF16)
    earlier = jnp.where(
        lax.broadcasted_iota(jnp.int32, (frame_count, frame_count), 0)
        < lax.broadcasted_iota(jnp.int32, (frame_count, frame_count), 1),
        1.0,
        0.0,
    ).astype(BF16)
    position = jnp.dot(named, earlier, preferred_element_type=F32)
    row0 = id0.astype(F32) * cap + jnp.sum(
        jnp.where(named0, position, 0.0), axis=0, keepdims=True
    )
    row1 = id1.astype(F32) * cap + jnp.sum(
        jnp.where(named1, position, 0.0), axis=0, keepdims=True
    )
    stacked = jnp.where(
        lane == 0,
        row0,
        jnp.where(
            lane == 1, row1, jnp.where(lane == 2, gates_ref[0:1, :], gates_ref[1:2, :])
        ),
    )
    turned[...] = jnp.transpose(stacked)
    row0 = row0.astype(jnp.int32)
    row1 = row1.astype(jnp.int32)

    def plane_of(g):
        return ((plane // 2 + g % 2) % 2) * 2 + (plane % 2 + g // 2) % 2

    def send_copy(p):
        return remote(
            outgoing.at[slots(p), :],
            arrived.at[slots(me_w), my_cols],
            fs.at[p],
            fr.at[me_w],
            (p, me_n),
        )

    def recv_copy(s):
        return remote(
            outgoing.at[slots(s), :],
            arrived.at[slots(s), my_cols],
            fs.at[s],
            fr.at[s],
            (s, me_n),
        )

    mine = frames_ref[:, my_cols]
    for turn, g in enumerate((1, 0, 3, 2)):
        q = plane_of(g)
        place = lax.broadcasted_iota(jnp.int32, (rows, frame_count), 0) + q * rows
        choose = jnp.where((place == row0) | (place == row1), 1.0, 0.0).astype(BF16)
        outgoing[group_rows(q), :] = jnp.dot(
            choose, mine, preferred_element_type=F32
        ).astype(BF16)
        if turn == 0:
            pl.semaphore_wait(barrier, wide - 1 + narrow - 1)
        if g == 0:
            arrived[slots(me_w), my_cols] = outgoing[slots(me_w), :]

        def send(i, carry, q=q):
            send_copy(q * size + (inner + i) % size).start()
            return carry

        if g < groups - 1:
            lax.fori_loop(1 if g == 0 else 0, size, send, 0)

    def forward_copy(g, q, m):
        part = arrived.at[group_rows(q), my_cols]
        return remote(part, part, xs.at[g, m], xr.at[g, me_n], (me_w, m))

    def forward_in(g, q, m):
        part = arrived.at[group_rows(q), cols(m)]
        return remote(part, part, xs.at[g, m], xr.at[g, m], (me_w, m))

    def partial_copy(g, q, m):
        return remote(
            partial.at[group_rows(q), cols(m)],
            partial_in.at[me_n, group_rows(q), :],
            ps.at[g, m],
            pr.at[g, me_n],
            (me_w, m),
        )

    def partial_wait(g, q, m):
        return remote(
            partial.at[group_rows(q), cols(m)],
            partial_in.at[m, group_rows(q), :],
            ps.at[g, m],
            pr.at[g, m],
            (me_w, m),
        )

    def return_copy(s):
        return remote(
            sums.at[slots(s), :],
            returned.at[slots(me_w), :],
            rs.at[s],
            rr.at[me_w],
            (s, me_n),
        )

    def return_wait(p):
        return remote(
            sums.at[slots(p), :],
            returned.at[slots(p), :],
            rs.at[p],
            rr.at[p],
            (p, me_n),
        )

    siblings = [(me_n + i) % narrow for i in range(1, narrow)]
    tile = min(512, units)

    def take_in(g):
        q = plane_of(g)

        def take(i, c):
            s = q * size + (inner + size - i) % size

            @pl.when(s != me_w)
            def _():
                recv_copy(s).wait_recv()

            return c

        lax.fori_loop(0, size, take, 0)
        for m in siblings:
            forward_copy(g, q, m).start()

        @pl.when(g == 1)
        def _():
            last = plane_of(groups - 1)

            def send(i, c):
                send_copy(last * size + (inner + i) % size).start()
                return c

            lax.fori_loop(0, size, send, 0)

    def give_back(g):
        q = plane_of(g)
        total = own[...]
        for m in siblings:
            partial_wait(g, q, m).wait_recv()
            total = total + partial_in[m, group_rows(q), :].astype(F32)
        sums[group_rows(q), :] = total.astype(BF16)

        def give(i, c):
            s = q * size + (inner + size - i) % size

            @pl.when(s != me_w)
            def _():
                return_copy(s).start()

            return c

        lax.fori_loop(0, size, give, 0)

    take_in(jnp.int32(0))
    for load in loads[:3]:
        load.wait()

    def step(g, carry):
        q = plane_of(g)
        for m in siblings:
            forward_in(g, q, m).wait_recv()
        x = arrived[group_rows(q), :]
        for f in range(0, units, tile):
            gate = jnp.dot(x, w_gate[:, f : f + tile], preferred_element_type=F32)
            up = jnp.dot(x, w_up[:, f : f + tile], preferred_element_type=F32)
            hidden[:, f : f + tile] = (gate * jax.nn.sigmoid(gate) * up).astype(BF16)

        @pl.when(g > 0)
        def _():
            give_back(g - 1)

        @pl.when(g < groups - 1)
        def _():
            take_in(g + 1)

        for m in siblings:
            partial[group_rows(q), cols(m)] = jnp.dot(
                hidden[...], w_down[:, cols(m)], preferred_element_type=F32
            ).astype(BF16)
            partial_copy(g, q, m).start()
        own[...] = jnp.dot(hidden[...], w_down[:, my_cols], preferred_element_type=F32)
        return carry

    lax.fori_loop(0, groups, step, 0)
    give_back(groups - 1)

    for load in loads[3:]:
        load.wait()

    def sort(i, c):
        r = pl.ds(pl.multiple_of(i * 64, 64), 64)
        pin[r, :channels] = pin_raw[r, 0, :]
        pin[r, channels:] = pin_raw[r, 1, :]
        return c

    lax.fori_loop(0, width // 64, sort, 0)
    returned[slots(me_w), :] = sums[slots(me_w), :]

    mix0[...] = jnp.zeros_like(mix0)
    mix1[...] = jnp.zeros_like(mix1)

    def combine(g, carry):
        q = plane_of(g)

        def take(i, c):
            p = q * size + (inner + i) % size

            @pl.when(p != me_w)
            def _():
                return_wait(p).wait_recv()

            return c

        lax.fori_loop(0, size, take, 0)
        place = lax.broadcasted_iota(jnp.int32, (frame_count, rows), 1) + q * rows
        block = returned[group_rows(q), :]
        mix0[...] += jnp.dot(
            jnp.where(place == turned[:, 0:1].astype(jnp.int32), 1.0, 0.0).astype(BF16), block, preferred_element_type=F32
        )
        mix1[...] += jnp.dot(
            jnp.where(place == turned[:, 1:2].astype(jnp.int32), 1.0, 0.0).astype(BF16), block, preferred_element_type=F32
        )
        return carry

    lax.fori_loop(0, groups, combine, 0)
    mixed[:, my_cols] = (
        turned[:, 2:3] * mix0[...] + turned[:, 3:4] * mix1[...]
    ).astype(BF16)

    def mix_copy(m):
        part = mixed.at[:, my_cols]
        return remote(part, part, ms.at[m], mr.at[me_n], (me_w, m))

    def mix_wait(m):
        part = mixed.at[:, cols(m)]
        return remote(part, part, ms.at[m], mr.at[m], (me_w, m))

    for m in siblings:
        mix_copy(m).start()
    for m in siblings:
        mix_wait(m).wait_recv()

    res = frames_ref[...].astype(F32) + mixed[...].astype(F32)
    residual[...] = res
    centered = res - jnp.mean(res, axis=1, keepdims=True)
    variance = jnp.mean(centered * centered, axis=1, keepdims=True)
    normed = (centered * lax.rsqrt(variance + 1e-05) * gain_ref[...] + bias_ref[...]).astype(BF16)
    value_half = jnp.dot(normed, pin[:, :channels], preferred_element_type=F32)
    gate_half = jnp.dot(normed, pin[:, channels:], preferred_element_type=F32)
    glu = (value_half * jax.nn.sigmoid(gate_half)).astype(BF16)
    padded[HALO : HALO + frame_count, :] = glu
    padded32[HALO : HALO + frame_count, :] = glu.astype(F32)

    end = HALO + frame_count
    to_left = remote(
        padded.at[HALO : 2 * HALO, :],
        padded.at[end : end + HALO, :],
        hs.at[0],
        hr.at[0],
        ((me_w + wide - 1) % wide, me_n),
    )
    to_right = remote(
        padded.at[frame_count:end, :],
        padded.at[0:HALO, :],
        hs.at[1],
        hr.at[1],
        ((me_w + 1) % wide, me_n),
    )
    has_left = me_w > 0
    has_right = me_w < wide - 1

    @pl.when(has_left)
    def _():
        to_left.start()

    @pl.when(has_right)
    def _():
        to_right.start()

    half = (taps - 1) // 2
    step_rows = 64

    def depthwise(starts):
        def strip(c, carry):
            lanes = pl.ds(pl.multiple_of(c * 128, 128), 128)
            kernel_taps = depth_ref[:, lanes].astype(F32)
            for start in starts:
                total = jnp.zeros((step_rows, 128), F32)
                for j in range(taps):
                    low = start + HALO - half + j
                    total = total + padded32[low : low + step_rows, lanes] * kernel_taps[j : j + 1, :]
                activated[start : start + step_rows, lanes] = (
                    total * jax.nn.sigmoid(total)
                ).astype(BF16)
            return carry

        lax.fori_loop(0, channels // 128, strip, 0)

    depthwise(range(step_rows, frame_count - step_rows, step_rows))

    @pl.when(has_right)
    def _():
        to_left.wait_recv()
        padded32[end : end + HALO, :] = padded[end : end + HALO, :].astype(F32)

    @pl.when(jnp.logical_not(has_right))
    def _():
        padded32[end : end + HALO, :] = jnp.zeros((HALO, channels), F32)

    @pl.when(has_left)
    def _():
        to_right.wait_recv()
        padded32[0:HALO, :] = padded[0:HALO, :].astype(F32)

    @pl.when(jnp.logical_not(has_left))
    def _():
        padded32[0:HALO, :] = jnp.zeros((HALO, channels), F32)

    depthwise((0, frame_count - step_rows))

    def share_copy(m):
        return remote(
            shares.at[share_rows(m), :], shares_in.at[me_n], os_.at[m], or_.at[me_n], (me_w, m)
        )

    def share_wait(m):
        return remote(
            shares.at[share_rows(m), :], shares_in.at[m], os_.at[m], or_.at[m], (me_w, m)
        )

    for m in siblings:
        shares[share_rows(m), :] = jnp.dot(
            activated[share_rows(m), :], pout[...], preferred_element_type=F32
        ).astype(BF16)
        share_copy(m).start()
    total = residual[share_rows(me_n), :] + jnp.dot(
        activated[share_rows(me_n), :], pout[...], preferred_element_type=F32
    )
    for m in siblings:
        share_wait(m).wait_recv()
        total = total + shares_in[m].astype(F32)
    out_ref[...] = total.astype(BF16)

    def finish(i, carry):
        p = (me_w + i) % wide
        send_copy(p).wait_send()
        return_copy(p).wait_send()
        return carry

    lax.fori_loop(1, wide, finish, 0)
    for m in siblings:
        mix_copy(m).wait_send()
        share_copy(m).wait_send()

    def finish_group(g, carry):
        q = plane_of(g)
        for m in siblings:
            forward_copy(g, q, m).wait_send()
            partial_copy(g, q, m).wait_send()
        return carry

    lax.fori_loop(0, groups, finish_group, 0)

    @pl.when(has_left)
    def _():
        to_left.wait_send()

    @pl.when(has_right)
    def _():
        to_right.wait_send()


def shards(
    frames,
    expert_ids,
    gate_values,
    w_gate,
    w_up,
    w_down,
    norm_gain,
    norm_bias,
    point_in,
    depth_kernel,
    point_out,
):
    frame_count, width = frames.shape
    top_count = expert_ids.shape[1]
    wide = lax.axis_size("wide")
    narrow = lax.axis_size("narrow")
    expert_count = w_gate.shape[0] * wide
    cap = 2 * top_count * frame_count // expert_count
    units = w_gate.shape[2]
    channels = point_in.shape[2]
    groups = 4
    slot_count = wide * cap
    rows = slot_count // groups
    dc = width // narrow
    share = frame_count // narrow
    vmem = pl.BlockSpec(memory_space=pltpu.VMEM)
    hbm = pl.BlockSpec(memory_space=pl.ANY)
    dma = pltpu.SemaphoreType.DMA
    flops = 2 * width * (3 * slot_count * units + 3 * frame_count * channels)
    return pl.pallas_call(
        functools.partial(block_kernel, wide, narrow, groups, cap),
        out_shape=jax.ShapeDtypeStruct((share, width), BF16),
        in_specs=[vmem] * 6 + [hbm] * 5,
        out_specs=vmem,
        scratch_shapes=[
            pltpu.VMEM((width, units), BF16),
            pltpu.VMEM((width, units), BF16),
            pltpu.VMEM((units, width), BF16),
            pltpu.VMEM((width, 2, channels), BF16),
            pltpu.VMEM((width, 2 * channels), BF16),
            pltpu.VMEM((channels, width), BF16),
            pltpu.VMEM((frame_count, 128), F32),
            pltpu.VMEM((rows, dc), F32),
            pltpu.VMEM((slot_count, dc), BF16),
            pltpu.VMEM((slot_count, width), BF16),
            pltpu.VMEM((rows, units), BF16),
            pltpu.VMEM((slot_count, width), BF16),
            pltpu.VMEM((narrow, slot_count, dc), BF16),
            pltpu.VMEM((slot_count, dc), BF16),
            pltpu.VMEM((slot_count, dc), BF16),
            pltpu.VMEM((frame_count, dc), F32),
            pltpu.VMEM((frame_count, dc), F32),
            pltpu.VMEM((frame_count, width), BF16),
            pltpu.VMEM((frame_count, width), F32),
            pltpu.VMEM((frame_count + 2 * HALO, channels), BF16),
            pltpu.VMEM((frame_count + 2 * HALO, channels), F32),
            pltpu.VMEM((frame_count, channels), BF16),
            pltpu.VMEM((frame_count, width), BF16),
            pltpu.VMEM((narrow, share, width), BF16),
            dma((5,)),
            dma((wide,)),
            dma((wide,)),
            dma((groups, narrow)),
            dma((groups, narrow)),
            dma((groups, narrow)),
            dma((groups, narrow)),
            dma((wide,)),
            dma((wide,)),
            dma((narrow,)),
            dma((narrow,)),
            dma((2,)),
            dma((2,)),
            dma((narrow,)),
            dma((narrow,)),
        ],
        compiler_params=pltpu.CompilerParams(
            collective_id=0, has_side_effects=True, vmem_limit_bytes=56 * 1024 * 1024
        ),
        cost_estimate=pl.CostEstimate(
            flops=flops, bytes_accessed=2 * 3 * width * units, transcendentals=0
        ),
        name="conformer_block",
    )(
        frames,
        expert_ids.T,
        gate_values.T,
        norm_gain.reshape(1, width),
        norm_bias.reshape(1, width),
        depth_kernel,
        w_gate,
        w_up,
        w_down,
        point_in,
        point_out,
    )


def solution(mesh):
    return jax.shard_map(
        shards,
        mesh=mesh,
        in_specs=(
            P("wide", None),
            P("wide", None),
            P("wide", None),
            P("wide", None, "narrow"),
            P("wide", None, "narrow"),
            P("wide", "narrow", None),
            P(),
            P(),
            P(None, None, "narrow"),
            P(None, "narrow"),
            P("narrow", None),
        ),
        out_specs=P(("wide", "narrow"), None),
        check_vma=False,
    )
```
